256 devices in a mesh: cells: 64 (over z_hi, y, x, core), tm: 4 (over z_lo).
Axes of the slice: x: 4, y: 4, z: 8 (z_hi: 2, z_lo: 4; z = z_hi * 4 + z_lo), core: 2. Of those that a mesh axis runs over, the one named last changes fastest.
Arguments:
- urban: float32 [2048, 8192], P('tm', 'cells')
- rural: float32 [2048, 8192], P('tm', 'cells')
- urban_valid: int32 [8192], P('cells'), may hold values from 1024 to 2048
- rural_ids: int32 [8, 8192], P(None, 'cells'), may hold values from 0 to 8191, as said below
Outputs:
- correlation: float32 [128, 8, 8192], P('tm', None, 'cells')
The draws below stay inside these ranges and needn't reach their ends.
Inputs may be any that keep to these rules, and one draw needn't show every extreme that they name: `rural_ids`: the rural cell with id i lies on index i // 128 of cells. Of the 1024 references of the urban cells of one index of cells, at most 16 name rural cells of any one other index, and for every index some other index has exactly 16.
All inputs are finite; a program needn't handle non-finite values.
Results may differ from the reference program's by a relative error of at most 0.0024.
Values may be sent and summed in bfloat16 or wider, within the bound.
A program may use at most 128 MiB of HBM per device.

```python
import jax
import jax.numpy as jnp
from jax import lax

K = 8
LAGS = 128
C_DEV = 128
R_DEV = 128
CAPF = 16
NH = 2048
NU = 8192
NR = 8192


def make_series(key, rows, cols):
    key_off, key_noise = jax.random.split(key, 2)
    offset = jax.random.uniform(key_off, (1, cols), jnp.float32, -2.0, 2.0)
    trend = 2.0 * jnp.arange(rows, dtype=jnp.float32)[:, None] / rows
    noise = jax.random.normal(key_noise, (rows, cols), jnp.float32)
    return offset + trend + noise


def draw_urban(key, part):
    return make_series(jax.random.fold_in(key, 11), NH, NU)


def draw_rural(key, part):
    return make_series(jax.random.fold_in(key, 23), NH, NR)


def draw_rural_ids(key, part):
    devices = NR // R_DEV
    capacity = CAPF
    slots_all = K * C_DEV
    key_count, key_force, key_perm, key_local = jax.random.split(key, 4)
    counts = jax.random.randint(key_count, (devices, devices), 1, capacity + 1)
    device_idx = jnp.arange(devices, dtype=jnp.int32)
    forced = jax.random.randint(key_force, (devices,), 0, devices - 1)
    other = (device_idx + 1 + forced) % devices
    counts = counts.at[device_idx, other].set(capacity)
    counts = jnp.where(device_idx[:, None] == device_idx[None, :], 0, counts)
    cumulative = jnp.cumsum(counts, axis=1)
    totals = cumulative[:, -1]
    slot_idx = jnp.arange(slots_all, dtype=jnp.int32)
    owners = jnp.sum((slot_idx[None, :, None] >= cumulative[:, None, :]).astype(jnp.int32), axis=2)
    owners = jnp.where(slot_idx[None, :] < totals[:, None], owners, device_idx[:, None])
    perm_keys = jax.random.split(key_perm, devices)
    orders = jax.vmap(lambda one_key: jax.random.permutation(one_key, slots_all))(perm_keys)
    owners = jnp.take_along_axis(owners, orders, axis=1)
    local_idx = jax.random.randint(key_local, (devices, slots_all), 0, R_DEV)
    ids_all = (owners * R_DEV + local_idx).astype(jnp.int32)
    return jnp.transpose(ids_all.reshape(devices, K, C_DEV), (1, 0, 2)).reshape(K, NU)


def with_ends(values, rng, least, largest):
    shape = values.shape
    place = [jax.random.randint(jax.random.fold_in(rng, axis), (), 0, shape[axis]) for axis in range(len(shape))]
    values = values.at[tuple(place)].set(least)
    longest = shape.index(max(shape))
    place[longest] = (place[longest] + 1) % shape[longest]
    return values.at[tuple(place)].set(largest)


def setup_inputs(seed: int = 0) -> dict:
    keys = jax.random.split(jax.random.key(seed), 5)
    urban = draw_urban(jax.random.fold_in(keys[4], 71), 0)
    rural = draw_rural(jax.random.fold_in(keys[4], 71), 0)
    urban_valid = with_ends(jax.random.randint(keys[2], (NU,), NH // 2, NH + 1), jax.random.fold_in(keys[2], 1), NH // 2, NH).astype(jnp.int32)
    rural_ids = draw_rural_ids(jax.random.fold_in(keys[4], 71), 0)
    return {"urban": urban, "rural": rural, "urban_valid": urban_valid, "rural_ids": rural_ids}


EPSILON = 1e-05

def standardize(series, valid_mask, valid_count):
    first_sum = lax.optimization_barrier(jnp.sum(series * valid_mask, axis=0))
    second_sum = lax.optimization_barrier(jnp.sum(series * series * valid_mask, axis=0))
    average = first_sum / valid_count
    spread = second_sum / valid_count - average * average
    return ((series - average) * lax.rsqrt(spread + EPSILON) * valid_mask).astype(jnp.bfloat16)

def reference(urban, rural, urban_valid, rural_ids):
    hour_idx = jnp.arange(NH, dtype=jnp.int32)[:, None]
    urban_mask = (hour_idx < urban_valid[None, :]).astype(jnp.float32)
    urban_z = standardize(urban, urban_mask, urban_valid.astype(jnp.float32))
    rural_z = standardize(rural, jnp.ones((1, 1), jnp.float32), jnp.float32(NH))
    offsets = jnp.arange(LAGS, dtype=jnp.int32)
    shift_idx = offsets[:, None] + offsets[None, :]

    def one_block(block_idx):
        first = block_idx * C_DEV
        urban_part = lax.dynamic_slice_in_dim(urban_z, first, C_DEV, 1)
        ids_part = lax.dynamic_slice_in_dim(rural_ids, first, C_DEV, 1)
        chosen = rural_z[:, ids_part]
        extended = jnp.concatenate([urban_part, jnp.zeros((LAGS - 1, C_DEV), urban_part.dtype)], 0)

        def step(total, hour_block):
            begin = hour_block * LAGS
            window = lax.dynamic_slice_in_dim(extended, begin, 2 * LAGS - 1, 0)
            toeplitz = window[shift_idx].astype(jnp.float32)
            refs = lax.dynamic_slice_in_dim(chosen, begin, LAGS, 0).astype(jnp.float32)
            return (total + jnp.einsum('skc,slc->lkc', refs, toeplitz), None)
        total, _ = lax.scan(step, jnp.zeros((LAGS, K, C_DEV), jnp.float32), jnp.arange(NH // LAGS, dtype=jnp.int32))
        return total
    blocks = lax.map(one_block, jnp.arange(NU // C_DEV, dtype=jnp.int32))
    totals = jnp.transpose(blocks, (1, 2, 0, 3)).reshape(LAGS, K, NU)
    intersection = (urban_valid[None, None, :] - offsets[:, None, None]).astype(jnp.float32)
    return totals / intersection
```

```python
import functools

import jax
import jax.numpy as jnp
from jax import lax
from jax.experimental import pallas as pl
from jax.experimental.pallas import tpu as pltpu
from jax.sharding import PartitionSpec as P

LAGS = 128
EPSILON = 1e-05
CAP = 16
GROUP = 32
MESH = pl.DeviceIdType.MESH
F32 = jnp.float32
BF16 = jnp.bfloat16

REQ, STAT, HALO, FETCH, PART = range(5)


def iota(shape, axis):
    return lax.broadcasted_iota(jnp.int32, shape, axis)


def bytes_wait(ref, sem):
    pltpu.make_async_copy(ref, ref, sem).wait()


def kernel(
    nc, nt, urban_ref, rural_ref, valid_ref, ids_ref, out_ref,
    req_out, req_in, req_acc, stats, ut, halo_out, halo_in, send, fetched, pick, toep, part, got, ssem, rsem,
):
    hours, cells = urban_ref.shape
    refs = ids_ref.shape[0]
    share = LAGS // nt
    groups = cells // GROUP
    wide = GROUP * refs
    slots = nc * CAP
    me = lax.axis_index("cells")
    tm = lax.axis_index("tm")

    def remote(kind, src, dst, **where):
        return pltpu.make_async_remote_copy(
            src_ref=src, dst_ref=dst, send_sem=ssem.at[kind], recv_sem=rsem.at[kind],
            device_id=where, device_id_type=MESH,
        )

    barrier = pltpu.get_barrier_semaphore()

    @pl.loop(1, nc)
    def _(d):
        pl.semaphore_signal(barrier, inc=1, device_id={"cells": lax.rem(me + d, nc)}, device_id_type=MESH)

    @pl.loop(1, nt)
    def _(d):
        pl.semaphore_signal(barrier, inc=1, device_id={"tm": lax.rem(tm + d, nt)}, device_id_type=MESH)

    valid = valid_ref[...].astype(F32)
    hour = (tm * hours + iota((hours, cells), 0)).astype(F32)
    mask = (hour < valid).astype(F32)
    urban = urban_ref[...]
    rural = rural_ref[...]
    mine = stats.at[tm]
    mine[0:1] = jnp.sum(urban * mask, axis=0, keepdims=True)
    mine[1:2] = jnp.sum(urban * urban * mask, axis=0, keepdims=True)
    mine[2:3] = jnp.sum(rural, axis=0, keepdims=True)
    mine[3:4] = jnp.sum(rural * rural, axis=0, keepdims=True)
    mine[4:8] = jnp.zeros((4, cells), F32)

    req_acc[...] = jnp.zeros_like(req_acc)
    ids = ids_ref[...]
    owners = (ids >> 7).astype(F32)
    lane = iota((GROUP, cells), 1)
    row = iota((GROUP, cells), 0)
    mef = me.astype(F32)

    @pl.loop(0, groups * refs)
    def _(block):
        g = block // refs
        k = block % refs
        one = (lane == GROUP * g + row)
        id_row = ids_ref[pl.ds(k, 1), :]
        owner = jnp.sum(jnp.where(one, (id_row >> 7).astype(F32), 0.0), axis=1, keepdims=True)
        local = jnp.sum(jnp.where(one, (id_row & 127).astype(F32), 0.0), axis=1, keepdims=True)
        place = k * cells + GROUP * g + row
        count = jnp.zeros((GROUP, cells), F32)
        for other in range(refs):
            earlier = (owners[other : other + 1] == owner) & (other * cells + lane < place)
            count += jnp.where(earlier, 1.0, 0.0)
        rank = jnp.sum(count, axis=1, keepdims=True)
        slot = jnp.where(owner == mef, slots + local, owner * CAP + rank).astype(jnp.int32)
        begin = pl.multiple_of(block * GROUP, GROUP)
        for j in range((slots + cells) // cells):
            hit = slot == lane + j * cells
            pick[pl.ds(begin, GROUP), j * cells : (j + 1) * cells] = jnp.where(hit, 1.0, 0.0).astype(BF16)
            if j < slots // cells:
                req_acc[:, j * cells : (j + 1) * cells] += jnp.where(hit, local, 0.0)

    asks = jnp.sum(req_acc[...], axis=0, keepdims=True).astype(jnp.int32)
    for j in range(slots // cells):
        req_out[j] = asks[:, j * cells : (j + 1) * cells]

    pl.semaphore_wait(barrier, nc - 1 + nt - 1)

    @pl.loop(1, nt)
    def _(d):
        remote(STAT, stats.at[tm], stats.at[tm], tm=lax.rem(tm + d, nt)).start()

    per = cells // CAP

    @pl.loop(1, nc)
    def _(d):
        peer = lax.rem(me + d, nc)
        remote(REQ, req_out.at[peer // per], req_in.at[me], cells=peer).start()

    req_in[me] = jnp.zeros((1, cells), jnp.int32)

    bytes_wait(stats.at[0 : nt - 1], rsem.at[STAT])
    total = stats[0]
    for i in range(1, nt):
        total += stats[i]

    def finish(series, first, second, n, keep):
        average = first / n
        spread = second / n - average * average
        return ((series - average) * lax.rsqrt(spread + EPSILON) * keep).astype(BF16).astype(F32)

    rural_z = finish(rural, total[2:3], total[3:4], F32(hours * nt), F32(1.0))
    rural_t = jnp.transpose(rural_z).astype(BF16)
    fetched[nc : nc + cells // CAP] = rural_t.reshape(cells // CAP, CAP, hours)
    urban_z = finish(urban, total[0:1], total[1:2], valid, mask)
    for j in range(hours // LAGS):
        ut[j] = jnp.transpose(urban_z[j * LAGS : (j + 1) * LAGS])
    halo_out[...] = ut[0].astype(BF16)

    @pl.when(tm > 0)
    def _():
        remote(HALO, halo_out, halo_in, tm=tm - 1).start()

    bytes_wait(req_in.at[0 : nc - 1], rsem.at[REQ])
    fetched[me] = jnp.zeros((CAP, hours), BF16)
    chunks = nc // per
    wanted = lax.rem(me, per) * CAP
    lane_c = iota((CAP, cells), 1)
    row_c = iota((CAP, cells), 0)
    here = lane_c == wanted + row_c

    @pl.loop(0, chunks)
    def _(step):
        q = lax.rem(me // per + step, chunks)
        columns = []
        for s in range(per):
            asked = req_in[q * per + s].astype(F32)
            columns.append(jnp.sum(jnp.where(here, asked, 0.0), axis=1, keepdims=True))
        column = jnp.concatenate(columns, axis=0).astype(jnp.int32)
        chosen = jnp.where(column == iota((cells, cells), 1), 1.0, 0.0).astype(BF16)
        rows = jnp.dot(chosen, fetched[nc : nc + cells // CAP].reshape(cells, hours), preferred_element_type=F32)
        send[pl.ds(q * per, per)] = rows.astype(BF16).reshape(per, CAP, hours)

        @pl.loop(0, per)
        def _(s):
            peer = q * per + s

            @pl.when(peer != me)
            def _():
                remote(FETCH, send.at[peer], fetched.at[me], cells=peer).start()

    @pl.when(tm < nt - 1)
    def _():
        bytes_wait(halo_in, rsem.at[HALO])
        ut[hours // LAGS] = halo_in[...].astype(F32)

    @pl.when(tm == nt - 1)
    def _():
        ut[hours // LAGS] = jnp.zeros((cells, LAGS), F32)

    tiles = hours // LAGS
    lane8 = iota((8, LAGS), 1)
    row8 = iota((8, LAGS), 0)

    @pl.loop(0, cells)
    def _(c):
        wave = [
            jnp.broadcast_to(ut[j, pl.ds(c, 1), :], (8, LAGS)) for j in range(tiles + 1)
        ]
        for pair in range(LAGS // 16):
            halves = []
            for a in (2 * pair, 2 * pair + 1):
                turned = [pltpu.roll(x, 8 * a + 1, 1, stride=1, stride_axis=0) for x in wave]
                upper = lane8 >= row8 + (8 * a + 1)
                halves.append([jnp.where(upper, turned[j + 1], turned[j]) for j in range(tiles)])
            for j in range(tiles):
                both = jnp.concatenate([halves[0][j], halves[1][j]], axis=0).astype(BF16)
                toep[c, 16 * pair : 16 * pair + 16, j * LAGS : (j + 1) * LAGS] = both

    bytes_wait(fetched.at[0 : nc - 1], rsem.at[FETCH])
    sub = 8
    column_of = lax.rem(iota((LAGS, wide), 1), GROUP)

    @pl.loop(0, groups)
    def _(g):
        begin = pl.multiple_of(g * wide, wide)
        weights = jnp.dot(
            pick[pl.ds(begin, wide), :],
            fetched[...].reshape(slots + cells, hours),
            preferred_element_type=F32,
        ).astype(BF16)
        part[g] = jnp.zeros((nt, share, wide), F32)

        @pl.loop(0, GROUP // sub)
        def _(b):
            first = b * sub
            left = toep[pl.ds(g * GROUP + first, sub)].reshape(sub * LAGS, hours)
            sums = lax.dot_general(left, weights, (((1,), (1,)), ((), ())), preferred_element_type=F32)
            total = part[g].reshape(LAGS, wide)
            for s in range(sub):
                total = jnp.where(column_of == first + s, sums[s * LAGS : (s + 1) * LAGS], total)
            part[g] = total.reshape(nt, share, wide)

        @pl.loop(1, nt)
        def _(d):
            peer = lax.rem(tm + d, nt)
            remote(PART, part.at[g, nt - 1 - peer], got.at[tm, g], tm=peer).start()

    got[tm] = part[:, nt - 1 - tm]
    bytes_wait(got.at[0 : nt - 1], rsem.at[PART])

    whole = []
    for g in range(groups):
        total = got[0, g]
        for i in range(1, nt):
            total += got[i, g]
        whole.append(total)
    lag = tm * share + (share - 1) - iota((share, cells), 0)
    overlap = (valid_ref[...] - lag).astype(F32)
    lane_o = iota((share, cells), 1)
    each = cells // GROUP
    for k in range(refs):
        tile = k // each
        result = jnp.zeros((share, cells), F32)
        for g in range(groups):
            piece = whole[g][:, tile * cells : (tile + 1) * cells]
            shift = (GROUP * (g - k % each)) % cells
            if shift:
                piece = pltpu.roll(piece, shift, 1)
            result = jnp.where(lane_o // GROUP == g, piece, result)
        result = result / overlap
        for i in range(share):
            out_ref[share - 1 - i, k : k + 1, :] = result[i : i + 1]

    bytes_wait(req_in.at[0 : nc - 1], ssem.at[REQ])
    bytes_wait(stats.at[0 : nt - 1], ssem.at[STAT])

    @pl.when(tm > 0)
    def _():
        bytes_wait(halo_out, ssem.at[HALO])

    bytes_wait(fetched.at[0 : nc - 1], ssem.at[FETCH])
    bytes_wait(got.at[0 : nt - 1], ssem.at[PART])


def solution(mesh):
    nc, nt = mesh.shape["cells"], mesh.shape["tm"]

    def shards(urban, rural, urban_valid, rural_ids):
        hours, cells = urban.shape
        refs = rural_ids.shape[0]
        share = LAGS // nt
        groups, wide, slots = cells // GROUP, GROUP * refs, nc * CAP
        return pl.pallas_call(
            functools.partial(kernel, nc, nt),
            out_shape=jax.ShapeDtypeStruct((share, refs, cells), F32),
            in_specs=[pl.BlockSpec(memory_space=pltpu.VMEM)] * 4,
            out_specs=pl.BlockSpec(memory_space=pltpu.VMEM),
            scratch_shapes=[
                pltpu.VMEM((slots // cells, 1, cells), jnp.int32),
                pltpu.VMEM((nc, 1, cells), jnp.int32),
                pltpu.VMEM((GROUP, slots), F32),
                pltpu.VMEM((nt, 8, cells), F32),
                pltpu.VMEM((hours // LAGS + 1, cells, LAGS), F32),
                pltpu.VMEM((cells, LAGS), BF16),
                pltpu.VMEM((cells, LAGS), BF16),
                pltpu.VMEM((nc, CAP, hours), BF16),
                pltpu.VMEM((nc + cells // CAP, CAP, hours), BF16),
                pltpu.VMEM((cells * refs, slots + cells), BF16),
                pltpu.VMEM((cells, LAGS, hours), BF16),
                pltpu.VMEM((groups, nt, share, wide), F32),
                pltpu.VMEM((nt, groups, share, wide), F32),
                pltpu.SemaphoreType.DMA((5,)),
                pltpu.SemaphoreType.DMA((5,)),
            ],
            compiler_params=pltpu.CompilerParams(
                collective_id=0, has_side_effects=True, vmem_limit_bytes=48 * 1024 * 1024
            ),
        )(urban, rural, urban_valid.reshape(1, cells), rural_ids)

    in_specs = (P("tm", "cells"), P("tm", "cells"), P("cells"), P(None, "cells"))
    return jax.shard_map(
        shards, mesh=mesh, in_specs=in_specs, out_specs=P("tm", None, "cells"), check_vma=False
    )
```

```python
import functools

import jax
import jax.numpy as jnp
from jax import lax
from jax.experimental import pallas as pl
from jax.experimental.pallas import tpu as pltpu
from jax.sharding import PartitionSpec as P

LAGS = 128
EPSILON = 1e-05
CAP = 16
GROUP = 32
PARTS = 2
MESH = pl.DeviceIdType.MESH
F32 = jnp.float32
BF16 = jnp.bfloat16

REQ, STAT, HALO, SUMS, TWIN, FETCH = 0, 1, 2, 3, 4, 4 + PARTS
KINDS = 4 + 2 * PARTS


def iota(shape, axis):
    return lax.broadcasted_iota(jnp.int32, shape, axis)


def bytes_wait(ref, sem):
    pltpu.make_async_copy(ref, ref, sem).wait()


def kernel(
    nc, nt, urban_hbm, rural_hbm, valid_ref, ids_ref, out_ref,
    urban_ref, rural_ref, req_out, req_in, req_acc, stats, ut, halo_out, halo_in,
    answer, choose, fetched, pick, toep, part, sums_out, sums_in, local_sem, ssem, rsem,
):
    hours, cells = urban_ref.shape
    refs = ids_ref.shape[0]
    share = LAGS // nt
    groups = cells // GROUP
    wide = GROUP * refs
    slots = nc * CAP
    half = nc // 2
    rows = cells // CAP
    span = hours // PARTS
    me = lax.axis_index("cells")
    tm = lax.axis_index("tm")
    side = me // half
    place = lax.rem(me, half)
    twin = (1 - side) * half + place

    def remote(kind, src, dst, **where):
        return pltpu.make_async_remote_copy(
            src_ref=src, dst_ref=dst, send_sem=ssem.at[kind], recv_sem=rsem.at[kind],
            device_id=where, device_id_type=MESH,
        )

    barrier = pltpu.get_barrier_semaphore()

    @pl.loop(1, nt)
    def _(d):
        pl.semaphore_signal(barrier, inc=1, device_id={"tm": lax.rem(tm + d, nt)}, device_id_type=MESH)

    pl.semaphore_signal(barrier, inc=1, device_id={"cells": twin}, device_id_type=MESH)

    @pl.loop(1, half)
    def _(d):
        peer = side * half + lax.rem(place + d, half)
        pl.semaphore_signal(barrier, inc=1, device_id={"cells": peer}, device_id_type=MESH)

    rural_in = pltpu.make_async_copy(rural_hbm, rural_ref, local_sem.at[0])
    urban_in = pltpu.make_async_copy(urban_hbm, urban_ref, local_sem.at[1])
    rural_in.start()
    urban_in.start()

    valid = valid_ref[...].astype(F32)
    hour = (tm * hours + iota((hours, cells), 0)).astype(F32)
    mask = (hour < valid).astype(F32)
    mine = stats.at[tm]
    rural_in.wait()
    rural = rural_ref[...]
    mine[2:3] = jnp.sum(rural, axis=0, keepdims=True)
    mine[3:4] = jnp.sum(rural * rural, axis=0, keepdims=True)
    urban_in.wait()
    urban = urban_ref[...]
    mine[0:1] = jnp.sum(urban * mask, axis=0, keepdims=True)
    mine[1:2] = jnp.sum(urban * urban * mask, axis=0, keepdims=True)
    mine[4:8] = jnp.zeros((4, cells), F32)

    pl.semaphore_wait(barrier, half - 1 + 1 + nt - 1)

    @pl.loop(1, nt)
    def _(d):
        remote(STAT, stats.at[tm], stats.at[tm], tm=lax.rem(tm + d, nt)).start()

    req_acc[...] = jnp.zeros_like(req_acc)
    owners = (ids_ref[...] >> 7).astype(F32)
    lane = iota((GROUP, cells), 1)
    row = iota((GROUP, cells), 0)
    mef = me.astype(F32)
    twinf = twin.astype(F32)
    sidef = side.astype(F32)

    @pl.loop(0, groups * refs, unroll=8)
    def _(block):
        g = block // refs
        k = block % refs
        one = lane == GROUP * g + row
        id_row = ids_ref[pl.ds(k, 1), :]
        owner = jnp.sum(jnp.where(one, (id_row >> 7).astype(F32), 0.0), axis=1, keepdims=True)
        local = jnp.sum(jnp.where(one, (id_row & 127).astype(F32), 0.0), axis=1, keepdims=True)
        order = k * cells + GROUP * g + row
        count = jnp.zeros((GROUP, cells), F32)
        for other in range(refs):
            earlier = (owners[other : other + 1] == owner) & (other * cells + lane < order)
            count += jnp.where(earlier, 1.0, 0.0)
        rank = jnp.sum(count, axis=1, keepdims=True)
        upper = jnp.where(owner >= half, 1.0, 0.0)
        away = jnp.where(upper == sidef, 0.0, 1.0)
        slot = ((owner - half * upper) * 2.0 + away) * CAP + rank
        slot = jnp.where(owner == mef, slots + local, jnp.where(owner == twinf, slots + cells + local, slot))
        slot = slot.astype(jnp.int32)
        begin = pl.multiple_of(block * GROUP, GROUP)
        for j in range(slots // cells + 2):
            hit = slot == lane + j * cells
            pick[pl.ds(begin, GROUP), j * cells : (j + 1) * cells] = jnp.where(hit, 1.0, 0.0).astype(BF16)
            if j < slots // cells:
                req_acc[:, j * cells : (j + 1) * cells] += jnp.where(hit, local, 0.0)

    asks = jnp.sum(req_acc[...], axis=0, keepdims=True).astype(jnp.int32)
    for j in range(slots // cells):
        req_out[j] = asks[:, j * cells : (j + 1) * cells]

    per = cells // (2 * CAP)

    @pl.loop(1, half)
    def _(d):
        other = lax.rem(place + d, half)
        remote(REQ, req_out.at[other // per], req_in.at[place], cells=side * half + other).start()

    req_in[place] = jnp.zeros((1, cells), jnp.int32)
    for p in range(PARTS):
        fetched[p, pl.ds(2 * place, 2)] = jnp.zeros((2, CAP, span), BF16)

    bytes_wait(stats.at[0 : nt - 1], rsem.at[STAT])
    total = stats[0]
    for i in range(1, nt):
        total += stats[i]

    def finish(series, first, second, n, keep):
        average = first / n
        spread = second / n - average * average
        return (series - average) * lax.rsqrt(spread + EPSILON) * keep

    rural_z = finish(rural_ref[...], total[2:3], total[3:4], F32(hours * nt), F32(1.0))
    for p in range(PARTS):
        turned = jnp.transpose(rural_z[p * span : (p + 1) * span]).astype(BF16)
        fetched[p, nc : nc + rows] = turned.reshape(rows, CAP, span)
        remote(
            TWIN + p, fetched.at[p, nc : nc + rows], fetched.at[p, nc + rows : nc + 2 * rows], cells=twin
        ).start()
    urban_z = finish(urban_ref[...], total[0:1], total[1:2], valid, mask)
    for j in range(hours // LAGS):
        ut[j] = jnp.transpose(urban_z[j * LAGS : (j + 1) * LAGS])
    halo_out[...] = ut[0].astype(BF16)

    @pl.when(tm > 0)
    def _():
        remote(HALO, halo_out, halo_in, tm=tm - 1).start()

    bytes_wait(req_in.at[0 : half - 1], rsem.at[REQ])
    batch = min(8, half)
    chunks = half // batch
    wanted = lax.rem(place, per) * 2 * CAP
    lane_c = iota((CAP, cells), 1)
    row_c = iota((CAP, cells), 0)
    here = [lane_c == wanted + rel * CAP + row_c for rel in range(2)]
    height = batch * CAP
    lane_h = iota((height, cells), 1)

    def respond(rel, p, q):
        block = fetched[p, nc + rel * rows : nc + (rel + 1) * rows].reshape(cells, span)
        begin = pl.multiple_of(q * height, height)
        chosen = jnp.dot(choose[rel, pl.ds(begin, height), :], block, preferred_element_type=F32)
        answer[p, rel, pl.ds(q * batch, batch)] = chosen.astype(BF16).reshape(batch, CAP, span)

        @pl.loop(0, batch)
        def _(s):
            other = q * batch + s

            @pl.when(other != place)
            def _():
                remote(
                    FETCH + p, answer.at[p, rel, other], fetched.at[p, 2 * place + rel], cells=side * half + other
                ).start()

    @pl.loop(0, chunks)
    def _(step):
        q = lax.rem(place // batch + step, chunks)
        begin = pl.multiple_of(q * height, height)
        for rel in range(2):
            columns = []
            for s in range(batch):
                asked = req_in[q * batch + s].astype(F32)
                columns.append(jnp.sum(jnp.where(here[rel], asked, 0.0), axis=1, keepdims=True))
            column = jnp.concatenate(columns, axis=0).astype(jnp.int32)
            choose[rel, pl.ds(begin, height), :] = jnp.where(column == lane_h, 1.0, 0.0).astype(BF16)
        for p in range(PARTS):
            respond(0, p, q)

    @pl.when(tm < nt - 1)
    def _():
        bytes_wait(halo_in, rsem.at[HALO])
        ut[hours // LAGS] = halo_in[...].astype(F32)

    @pl.when(tm == nt - 1)
    def _():
        ut[hours // LAGS] = jnp.zeros((cells, LAGS), F32)

    tiles = hours // LAGS
    lane8 = iota((8, LAGS), 1)
    row8 = iota((8, LAGS), 0)

    def build(first, last):
        @pl.loop(first, last, unroll=8)
        def _(c):
            wave = [jnp.broadcast_to(ut[j, pl.ds(c, 1), :], (8, LAGS)) for j in range(tiles + 1)]
            for pair in range(LAGS // 16):
                halves = []
                for a in (2 * pair, 2 * pair + 1):
                    turned = [pltpu.roll(x, 8 * a + 1, 1, stride=1, stride_axis=0) for x in wave]
                    upper = lane8 >= row8 + (8 * a + 1)
                    halves.append([jnp.where(upper, turned[j + 1], turned[j]) for j in range(tiles)])
                for j in range(tiles):
                    both = jnp.concatenate([halves[0][j], halves[1][j]], axis=0).astype(BF16)
                    at = (j * LAGS) % span
                    toep[(j * LAGS) // span, c, 16 * pair : 16 * pair + 16, at : at + LAGS] = both

    build(0, cells // 2)
    for p in range(PARTS):
        bytes_wait(fetched.at[p, nc + rows : nc + 2 * rows], rsem.at[TWIN + p])

        @pl.loop(0, chunks)
        def _(step):
            respond(1, p, lax.rem(place // batch + step, chunks))

    build(cells // 2, cells)

    column_of = lax.rem(iota((LAGS, wide), 1), GROUP)
    for p in range(PARTS):
        bytes_wait(fetched.at[p, 0 : nc - 2], rsem.at[FETCH + p])

        @pl.loop(0, groups)
        def _(g):
            begin = pl.multiple_of(g * wide, wide)
            weights = jnp.dot(
                pick[pl.ds(begin, wide), :],
                fetched[p].reshape(slots + 2 * cells, span),
                preferred_element_type=F32,
            ).astype(BF16)
            left = toep[p, pl.ds(g * GROUP, GROUP)].reshape(GROUP * LAGS, span)
            sums = lax.dot_general(left, weights, (((1,), (1,)), ((), ())), preferred_element_type=F32)
            total = sums[0:LAGS]
            for s in range(1, GROUP):
                total = jnp.where(column_of == s, sums[s * LAGS : (s + 1) * LAGS], total)
            if p:
                total += part[g].reshape(LAGS, wide)
            part[g] = total.reshape(nt, share, wide)
            if p == PARTS - 1:
                sums_out[g] = total.astype(BF16).reshape(nt, share, wide)

                @pl.loop(1, nt)
                def _(d):
                    peer = lax.rem(tm + d, nt)
                    remote(SUMS, sums_out.at[g, nt - 1 - peer], sums_in.at[tm, g], tm=peer).start()

    sums_in[tm] = jnp.zeros((groups, share, wide), BF16)
    bytes_wait(sums_in.at[0 : nt - 1], rsem.at[SUMS])

    whole = []
    for g in range(groups):
        total = part[g, nt - 1 - tm]
        for i in range(nt):
            total += sums_in[i, g].astype(F32)
        whole.append(total)
    lag = tm * share + (share - 1) - iota((share, cells), 0)
    overlap = (valid_ref[...] - lag).astype(F32)
    lane_o = iota((share, cells), 1)
    each = cells // GROUP
    for k in range(refs):
        tile = k // each
        result = jnp.zeros((share, cells), F32)
        for g in range(groups):
            piece = whole[g][:, tile * cells : (tile + 1) * cells]
            shift = (GROUP * (g - k % each)) % cells
            if shift:
                piece = pltpu.roll(piece, shift, 1)
            result = jnp.where(lane_o // GROUP == g, piece, result)
        result = result / overlap
        for i in range(share):
            out_ref[share - 1 - i, k : k + 1, :] = result[i : i + 1]

    bytes_wait(req_in.at[0 : half - 1], ssem.at[REQ])
    bytes_wait(stats.at[0 : nt - 1], ssem.at[STAT])

    @pl.when(tm > 0)
    def _():
        bytes_wait(halo_out, ssem.at[HALO])

    for p in range(PARTS):
        bytes_wait(fetched.at[p, nc : nc + rows], ssem.at[TWIN + p])
        bytes_wait(fetched.at[p, 0 : nc - 2], ssem.at[FETCH + p])
    bytes_wait(sums_in.at[0 : nt - 1], ssem.at[SUMS])


def solution(mesh):
    nc, nt = mesh.shape["cells"], mesh.shape["tm"]

    def shards(urban, rural, urban_valid, rural_ids):
        hours, cells = urban.shape
        refs = rural_ids.shape[0]
        share = LAGS // nt
        groups, wide, slots, half = cells // GROUP, GROUP * refs, nc * CAP, nc // 2
        span, rows = hours // PARTS, cells // CAP
        vmem = pl.BlockSpec(memory_space=pltpu.VMEM)
        whole = pl.BlockSpec(memory_space=pl.ANY)
        return pl.pallas_call(
            functools.partial(kernel, nc, nt),
            out_shape=jax.ShapeDtypeStruct((share, refs, cells), F32),
            in_specs=[whole, whole, vmem, vmem],
            out_specs=vmem,
            scratch_shapes=[
                pltpu.VMEM((hours, cells), F32),
                pltpu.VMEM((hours, cells), F32),
                pltpu.VMEM((slots // cells, 1, cells), jnp.int32),
                pltpu.VMEM((half, 1, cells), jnp.int32),
                pltpu.VMEM((GROUP, slots), F32),
                pltpu.VMEM((nt, 8, cells), F32),
                pltpu.VMEM((hours // LAGS + 1, cells, LAGS), F32),
                pltpu.VMEM((cells, LAGS), BF16),
                pltpu.VMEM((cells, LAGS), BF16),
                pltpu.VMEM((PARTS, 2, half, CAP, span), BF16),
                pltpu.VMEM((2, half * CAP, cells), BF16),
                pltpu.VMEM((PARTS, nc + 2 * rows, CAP, span), BF16),
                pltpu.VMEM((cells * refs, slots + 2 * cells), BF16),
                pltpu.VMEM((PARTS, cells, LAGS, span), BF16),
                pltpu.VMEM((groups, nt, share, wide), F32),
                pltpu.VMEM((groups, nt, share, wide), BF16),
                pltpu.VMEM((nt, groups, share, wide), BF16),
                pltpu.SemaphoreType.DMA((2,)),
                pltpu.SemaphoreType.DMA((KINDS,)),
                pltpu.SemaphoreType.DMA((KINDS,)),
            ],
            compiler_params=pltpu.CompilerParams(
                collective_id=0, has_side_effects=True, vmem_limit_bytes=52 * 1024 * 1024
            ),
        )(urban, rural, urban_valid.reshape(1, cells), rural_ids)

    in_specs = (P("tm", "cells"), P("tm", "cells"), P("cells"), P(None, "cells"))
    return jax.shard_map(
        shards, mesh=mesh, in_specs=in_specs, out_specs=P("tm", None, "cells"), check_vma=False
    )
```

```python
import functools

import jax
import jax.numpy as jnp
from jax import lax
from jax.experimental import pallas as pl
from jax.experimental.pallas import tpu as pltpu
from jax.sharding import PartitionSpec as P

LAGS = 128
EPSILON = 1e-05
CAP = 16
GROUP = 32
PARTS = 2
MESH = pl.DeviceIdType.MESH
F32 = jnp.float32
BF16 = jnp.bfloat16

REQ, STAT, HALO, SUMS, PEAK, TWIN, FETCH = 0, 1, 2, 3, 4, 5, 5 + PARTS
KINDS = 5 + 2 * PARTS
TOP = 32760.0


def iota(shape, axis):
    return lax.broadcasted_iota(jnp.int32, shape, axis)


def bytes_wait(ref, sem):
    pltpu.make_async_copy(ref, ref, sem).wait()


def kernel(
    nc, nt, urban_hbm, rural_hbm, valid_ref, ids_ref, out_ref,
    urban_ref, rural_ref, req_out, req_in, slot_rows, stats, ut, halo_out, halo_in,
    answer, choose, fetched, pick, toep, part, sums_out, sums_in, peak_out, peak_in, local_sem, ssem, rsem,
):
    hours, cells = urban_ref.shape
    refs = ids_ref.shape[0]
    share = LAGS // nt
    groups = cells // GROUP
    wide = GROUP * refs
    slots = nc * CAP
    half = nc // 2
    rows = cells // CAP
    span = hours // PARTS
    me = lax.axis_index("cells")
    tm = lax.axis_index("tm")
    side = me // half
    place = lax.rem(me, half)
    twin = (1 - side) * half + place

    def remote(kind, src, dst, **where):
        return pltpu.make_async_remote_copy(
            src_ref=src, dst_ref=dst, send_sem=ssem.at[kind], recv_sem=rsem.at[kind],
            device_id=where, device_id_type=MESH,
        )

    barrier = pltpu.get_barrier_semaphore()

    @pl.loop(1, nt)
    def _(d):
        pl.semaphore_signal(barrier, inc=1, device_id={"tm": lax.rem(tm + d, nt)}, device_id_type=MESH)

    pl.semaphore_signal(barrier, inc=1, device_id={"cells": twin}, device_id_type=MESH)

    @pl.loop(1, half)
    def _(d):
        peer = side * half + lax.rem(place + d, half)
        pl.semaphore_signal(barrier, inc=1, device_id={"cells": peer}, device_id_type=MESH)

    rural_in = pltpu.make_async_copy(rural_hbm, rural_ref, local_sem.at[0])
    urban_in = pltpu.make_async_copy(urban_hbm, urban_ref, local_sem.at[1])
    rural_in.start()
    urban_in.start()

    ids = ids_ref[...]
    owner = (ids >> 7).astype(F32)
    local = (ids & 127).astype(F32)
    upper = jnp.where(owner >= half, 1.0, 0.0)
    away = jnp.where(upper == side.astype(F32), 0.0, 1.0)
    home = (owner - half * upper) * 2.0 + away
    home_i = iota((nc, cells), 0).astype(F32)
    belongs = [jnp.where(home[k : k + 1] == home_i, 1.0, 0.0) for k in range(refs)]
    earlier = iota((cells, 2 * cells), 0) < iota((cells, 2 * cells), 1)
    counts = jnp.dot(
        jnp.concatenate(belongs, axis=0).astype(BF16), jnp.where(earlier, 1.0, 0.0).astype(BF16),
        preferred_element_type=F32,
    )
    before = jnp.zeros((nc, cells), F32)
    rank_i = iota((cells, cells), 0).astype(F32)
    asks = jnp.zeros((nc, cells), F32)
    for k in range(refs):
        count = counts[k * nc : (k + 1) * nc]
        rank = jnp.sum(belongs[k] * (count[:, 0:cells] + before), axis=0, keepdims=True)
        before += count[:, cells : 2 * cells]
        wish = jnp.where(rank == rank_i, local[k : k + 1], 0.0).astype(BF16)
        asks += lax.dot_general(
            belongs[k].astype(BF16), wish, (((1,), (1,)), ((), ())), preferred_element_type=F32
        )
        slot = home[k : k + 1] * CAP + rank
        slot = jnp.where(owner[k : k + 1] == me.astype(F32), slots + local[k : k + 1], slot)
        slot = jnp.where(owner[k : k + 1] == twin.astype(F32), slots + cells + local[k : k + 1], slot)
        slot_rows[k : k + 1] = slot
    asks = asks.astype(jnp.int32)
    for q in range(half):
        req_out[q] = asks[2 * q : 2 * q + 2]

    valid = valid_ref[...].astype(F32)
    hour = (tm * hours + iota((hours, cells), 0)).astype(F32)
    mask = (hour < valid).astype(F32)
    mine = stats.at[tm]
    rural_in.wait()
    rural = rural_ref[...]
    mine[2:3] = jnp.sum(rural, axis=0, keepdims=True)
    mine[3:4] = jnp.sum(rural * rural, axis=0, keepdims=True)
    urban_in.wait()
    urban = urban_ref[...]
    mine[0:1] = jnp.sum(urban * mask, axis=0, keepdims=True)
    mine[1:2] = jnp.sum(urban * urban * mask, axis=0, keepdims=True)
    mine[4:8] = jnp.zeros((4, cells), F32)

    pl.semaphore_wait(barrier, half - 1 + 1 + nt - 1)

    @pl.loop(1, nt)
    def _(d):
        remote(STAT, stats.at[tm], stats.at[tm], tm=lax.rem(tm + d, nt)).start()


    @pl.loop(1, half)
    def _(d):
        other = lax.rem(place + d, half)
        remote(REQ, req_out.at[other], req_in.at[place], cells=side * half + other).start()

    req_in[place] = jnp.zeros((2, cells), jnp.int32)

    lane = iota((GROUP, cells), 1)
    row = iota((GROUP, cells), 0)

    @pl.loop(0, groups * refs, unroll=8)
    def _(block):
        one = lane == GROUP * (block // refs) + row
        slot_row = slot_rows[pl.ds(block % refs, 1), :]
        slot = jnp.sum(jnp.where(one, slot_row, 0.0), axis=1, keepdims=True).astype(jnp.int32)
        begin = pl.multiple_of(block * GROUP, GROUP)
        for j in range(slots // cells + 2):
            hit = slot == lane + j * cells
            pick[pl.ds(begin, GROUP), j * cells : (j + 1) * cells] = jnp.where(hit, 1.0, 0.0).astype(BF16)

    for p in range(PARTS):
        fetched[p, pl.ds(2 * place, 2)] = jnp.zeros((2, CAP, span), BF16)

    bytes_wait(stats.at[0 : nt - 1], rsem.at[STAT])
    total = stats[0]
    for i in range(1, nt):
        total += stats[i]

    def finish(series, first, second, n, keep):
        average = first / n
        spread = second / n - average * average
        return (series - average) * lax.rsqrt(spread + EPSILON) * keep

    rural_z = finish(rural_ref[...], total[2:3], total[3:4], F32(hours * nt), F32(1.0))
    for p in range(PARTS):
        turned = jnp.transpose(rural_z[p * span : (p + 1) * span]).astype(BF16)
        fetched[p, nc : nc + rows] = turned.reshape(rows, CAP, span)
        remote(
            TWIN + p, fetched.at[p, nc : nc + rows], fetched.at[p, nc + rows : nc + 2 * rows], cells=twin
        ).start()
    urban_z = finish(urban_ref[...], total[0:1], total[1:2], valid, mask)
    for j in range(hours // LAGS):
        ut[j] = jnp.transpose(urban_z[j * LAGS : (j + 1) * LAGS])
    halo_out[...] = ut[0].astype(BF16)

    @pl.when(tm > 0)
    def _():
        remote(HALO, halo_out, halo_in, tm=tm - 1).start()

    bytes_wait(req_in.at[0 : half - 1], rsem.at[REQ])
    batch = min(8, half)
    chunks = half // batch
    lane_c = iota((CAP, cells), 1)
    row_c = iota((CAP, cells), 0)
    here = lane_c == row_c
    height = batch * CAP
    lane_h = iota((height, cells), 1)

    def respond(rel, p, q):
        block = fetched[p, nc + rel * rows : nc + (rel + 1) * rows].reshape(cells, span)
        begin = pl.multiple_of(q * height, height)
        chosen = jnp.dot(choose[rel, pl.ds(begin, height), :], block, preferred_element_type=F32)
        answer[p, rel, pl.ds(q * batch, batch)] = chosen.astype(BF16).reshape(batch, CAP, span)

        @pl.loop(0, batch)
        def _(s):
            other = q * batch + s

            @pl.when(other != place)
            def _():
                remote(
                    FETCH + p, answer.at[p, rel, other], fetched.at[p, 2 * place + rel], cells=side * half + other
                ).start()

    def respond_all(rel, p):
        @pl.loop(0, chunks)
        def _(step):
            respond(rel, p, lax.rem(place // batch + step, chunks))

    @pl.loop(0, chunks)
    def _(step):
        q = lax.rem(place // batch + step, chunks)
        begin = pl.multiple_of(q * height, height)
        for rel in range(2):
            columns = []
            for s in range(batch):
                asked = req_in[q * batch + s][rel : rel + 1].astype(F32)
                columns.append(jnp.sum(jnp.where(here, asked, 0.0), axis=1, keepdims=True))
            column = jnp.concatenate(columns, axis=0).astype(jnp.int32)
            choose[rel, pl.ds(begin, height), :] = jnp.where(column == lane_h, 1.0, 0.0).astype(BF16)
        respond(0, 0, q)

    for p in range(1, PARTS):
        respond_all(0, p)

    @pl.when(tm < nt - 1)
    def _():
        bytes_wait(halo_in, rsem.at[HALO])
        ut[hours // LAGS] = halo_in[...].astype(F32)

    @pl.when(tm == nt - 1)
    def _():
        ut[hours // LAGS] = jnp.zeros((cells, LAGS), F32)

    tiles = hours // LAGS
    lane8 = iota((8, LAGS), 1)
    row8 = iota((8, LAGS), 0)

    def build(first, last):
        @pl.loop(first, last, unroll=8)
        def _(c):
            wave = [jnp.broadcast_to(ut[j, pl.ds(c, 1), :], (8, LAGS)) for j in range(tiles + 1)]
            for pair in range(LAGS // 16):
                halves = []
                for a in (2 * pair, 2 * pair + 1):
                    turned = [pltpu.roll(x, 8 * a + 1, 1, stride=1, stride_axis=0) for x in wave]
                    upper = lane8 >= row8 + (8 * a + 1)
                    halves.append([jnp.where(upper, turned[j + 1], turned[j]) for j in range(tiles)])
                for j in range(tiles):
                    both = jnp.concatenate([halves[0][j], halves[1][j]], axis=0).astype(BF16)
                    at = (j * LAGS) % span
                    toep[(j * LAGS) // span, c, 16 * pair : 16 * pair + 16, at : at + LAGS] = both

    step = cells // (2 * PARTS)
    for p in range(PARTS):
        build(p * step, (p + 1) * step)
        bytes_wait(fetched.at[p, nc + rows : nc + 2 * rows], rsem.at[TWIN + p])
        respond_all(1, p)

    build(cells // 2, cells)

    column_of = lax.rem(iota((LAGS, wide), 1), GROUP)
    for p in range(PARTS):
        bytes_wait(fetched.at[p, 0 : nc - 2], rsem.at[FETCH + p])

        @pl.loop(0, groups)
        def _(g):
            begin = pl.multiple_of(g * wide, wide)
            weights = jnp.dot(
                pick[pl.ds(begin, wide), :],
                fetched[p].reshape(slots + 2 * cells, span),
                preferred_element_type=F32,
            ).astype(BF16)
            left = toep[p, pl.ds(g * GROUP, GROUP)].reshape(GROUP * LAGS, span)
            sums = lax.dot_general(left, weights, (((1,), (1,)), ((), ())), preferred_element_type=F32)
            total = sums[0:LAGS]
            for s in range(1, GROUP):
                total = jnp.where(column_of == s, sums[s * LAGS : (s + 1) * LAGS], total)
            if p:
                total += part[g].reshape(LAGS, wide)
            part[g] = total.reshape(nt, share, wide)
            if p == PARTS - 1:
                peak = jnp.maximum(jnp.max(jnp.abs(total), axis=0, keepdims=True), 1e-30)
                peak_out[g] = peak
                coded = jnp.floor(total * (TOP / peak) + 0.5).astype(jnp.int32).astype(jnp.int16)
                sums_out[g] = coded.reshape(nt, share, wide)

                @pl.loop(1, nt)
                def _(d):
                    peer = lax.rem(tm + d, nt)
                    remote(SUMS, sums_out.at[g, nt - 1 - peer], sums_in.at[tm, g], tm=peer).start()
                    remote(PEAK, peak_out.at[g], peak_in.at[tm, g], tm=peer).start()

    sums_in[tm] = jnp.zeros((groups, share, wide), jnp.int16)
    peak_in[tm] = jnp.zeros((groups, 1, wide), F32)
    bytes_wait(sums_in.at[0 : nt - 1], rsem.at[SUMS])
    bytes_wait(peak_in.at[0 : nt - 1], rsem.at[PEAK])

    whole = []
    for g in range(groups):
        total = part[g, nt - 1 - tm]
        for i in range(nt):
            total += sums_in[i, g].astype(jnp.int32).astype(F32) * (peak_in[i, g] * (1.0 / TOP))
        whole.append(total)
    lag = tm * share + (share - 1) - iota((share, cells), 0)
    overlap = (valid_ref[...] - lag).astype(F32)
    lane_o = iota((share, cells), 1)
    each = cells // GROUP
    for k in range(refs):
        tile = k // each
        result = jnp.zeros((share, cells), F32)
        for g in range(groups):
            piece = whole[g][:, tile * cells : (tile + 1) * cells]
            shift = (GROUP * (g - k % each)) % cells
            if shift:
                piece = pltpu.roll(piece, shift, 1)
            result = jnp.where(lane_o // GROUP == g, piece, result)
        result = result / overlap
        for i in range(share):
            out_ref[share - 1 - i, k : k + 1, :] = result[i : i + 1]

    bytes_wait(req_in.at[0 : half - 1], ssem.at[REQ])
    bytes_wait(stats.at[0 : nt - 1], ssem.at[STAT])

    @pl.when(tm > 0)
    def _():
        bytes_wait(halo_out, ssem.at[HALO])

    for p in range(PARTS):
        bytes_wait(fetched.at[p, nc : nc + rows], ssem.at[TWIN + p])
        bytes_wait(fetched.at[p, 0 : nc - 2], ssem.at[FETCH + p])
    bytes_wait(sums_in.at[0 : nt - 1], ssem.at[SUMS])
    bytes_wait(peak_in.at[0 : nt - 1], ssem.at[PEAK])


def solution(mesh):
    nc, nt = mesh.shape["cells"], mesh.shape["tm"]

    def shards(urban, rural, urban_valid, rural_ids):
        hours, cells = urban.shape
        refs = rural_ids.shape[0]
        share = LAGS // nt
        groups, wide, slots, half = cells // GROUP, GROUP * refs, nc * CAP, nc // 2
        span, rows = hours // PARTS, cells // CAP
        vmem = pl.BlockSpec(memory_space=pltpu.VMEM)
        whole = pl.BlockSpec(memory_space=pl.ANY)
        return pl.pallas_call(
            functools.partial(kernel, nc, nt),
            out_shape=jax.ShapeDtypeStruct((share, refs, cells), F32),
            in_specs=[whole, whole, vmem, vmem],
            out_specs=vmem,
            scratch_shapes=[
                pltpu.VMEM((hours, cells), F32),
                pltpu.VMEM((hours, cells), F32),
                pltpu.VMEM((half, 2, cells), jnp.int32),
                pltpu.VMEM((half, 2, cells), jnp.int32),
                pltpu.VMEM((refs, cells), F32),
                pltpu.VMEM((nt, 8, cells), F32),
                pltpu.VMEM((hours // LAGS + 1, cells, LAGS), F32),
                pltpu.VMEM((cells, LAGS), BF16),
                pltpu.VMEM((cells, LAGS), BF16),
                pltpu.VMEM((PARTS, 2, half, CAP, span), BF16),
                pltpu.VMEM((2, half * CAP, cells), BF16),
                pltpu.VMEM((PARTS, nc + 2 * rows, CAP, span), BF16),
                pltpu.VMEM((cells * refs, slots + 2 * cells), BF16),
                pltpu.VMEM((PARTS, cells, LAGS, span), BF16),
                pltpu.VMEM((groups, nt, share, wide), F32),
                pltpu.VMEM((groups, nt, share, wide), jnp.int16),
                pltpu.VMEM((nt, groups, share, wide), jnp.int16),
                pltpu.VMEM((groups, 1, wide), F32),
                pltpu.VMEM((nt, groups, 1, wide), F32),
                pltpu.SemaphoreType.DMA((2,)),
                pltpu.SemaphoreType.DMA((KINDS,)),
                pltpu.SemaphoreType.DMA((KINDS,)),
            ],
            compiler_params=pltpu.CompilerParams(
                collective_id=0, has_side_effects=True, vmem_limit_bytes=52 * 1024 * 1024
            ),
        )(urban, rural, urban_valid.reshape(1, cells), rural_ids)

    in_specs = (P("tm", "cells"), P("tm", "cells"), P("cells"), P(None, "cells"))
    return jax.shard_map(
        shards, mesh=mesh, in_specs=in_specs, out_specs=P("tm", None, "cells"), check_vma=False
    )
```

```python
import functools

import jax
import jax.numpy as jnp
from jax import lax
from jax.experimental import pallas as pl
from jax.experimental.pallas import tpu as pltpu
from jax.sharding import PartitionSpec as P

LAGS = 128
EPSILON = 1e-05
CAP = 16
GROUP = 8
PARTS = 2
MESH = pl.DeviceIdType.MESH
F32 = jnp.float32
BF16 = jnp.bfloat16

REQ, STAT, HALO, SUMS, PEAK, TWIN, FETCH = 0, 1, 2, 3, 4, 5, 5 + PARTS
KINDS = 5 + 2 * PARTS
TOP = 32760.0


def iota(shape, axis):
    return lax.broadcasted_iota(jnp.int32, shape, axis)


def bytes_wait(ref, sem):
    pltpu.make_async_copy(ref, ref, sem).wait()


def kernel(
    nc, nt, urban_hbm, rural_hbm, valid_ref, ids_ref, out_ref,
    urban_ref, rural_ref, req_out, req_in, slot_rows, stats, ut, halo_out, halo_in,
    answer, choose, fetched, pick, toep, moved, part, kept, sums_out, sums_in, peak_out, peak_in, local_sem, ssem, rsem,
):
    hours, cells = urban_ref.shape
    refs = ids_ref.shape[0]
    share = LAGS // nt
    groups = cells // GROUP
    wide = GROUP * refs
    quads = groups // 4
    slots = nc * CAP
    half = nc // 2
    rows = cells // CAP
    span = hours // PARTS
    me = lax.axis_index("cells")
    tm = lax.axis_index("tm")
    side = me // half
    place = lax.rem(me, half)
    twin = (1 - side) * half + place

    def remote(kind, src, dst, **where):
        return pltpu.make_async_remote_copy(
            src_ref=src, dst_ref=dst, send_sem=ssem.at[kind], recv_sem=rsem.at[kind],
            device_id=where, device_id_type=MESH,
        )

    barrier = pltpu.get_barrier_semaphore()

    @pl.loop(1, nt)
    def _(d):
        pl.semaphore_signal(barrier, inc=1, device_id={"tm": lax.rem(tm + d, nt)}, device_id_type=MESH)

    pl.semaphore_signal(barrier, inc=1, device_id={"cells": twin}, device_id_type=MESH)

    @pl.loop(1, half)
    def _(d):
        peer = side * half + lax.rem(place + d, half)
        pl.semaphore_signal(barrier, inc=1, device_id={"cells": peer}, device_id_type=MESH)

    rural_in = pltpu.make_async_copy(rural_hbm, rural_ref, local_sem.at[0])
    urban_in = pltpu.make_async_copy(urban_hbm, urban_ref, local_sem.at[1])
    rural_in.start()
    urban_in.start()

    ids = ids_ref[...]
    owner = (ids >> 7).astype(F32)
    local = (ids & 127).astype(F32)
    upper = jnp.where(owner >= half, 1.0, 0.0)
    away = jnp.where(upper == side.astype(F32), 0.0, 1.0)
    home = (owner - half * upper) * 2.0 + away
    home_i = iota((nc, cells), 0).astype(F32)
    belongs = [jnp.where(home[k : k + 1] == home_i, 1.0, 0.0) for k in range(refs)]
    earlier = iota((cells, 2 * cells), 0) < iota((cells, 2 * cells), 1)
    counts = jnp.dot(
        jnp.concatenate(belongs, axis=0).astype(BF16), jnp.where(earlier, 1.0, 0.0).astype(BF16),
        preferred_element_type=F32,
    )
    before = jnp.zeros((nc, cells), F32)
    rank_i = iota((cells, cells), 0).astype(F32)
    asks = jnp.zeros((nc, cells), F32)
    for k in range(refs):
        count = counts[k * nc : (k + 1) * nc]
        rank = jnp.sum(belongs[k] * (count[:, 0:cells] + before), axis=0, keepdims=True)
        before += count[:, cells : 2 * cells]
        wish = jnp.where(rank == rank_i, local[k : k + 1], 0.0).astype(BF16)
        asks += lax.dot_general(
            belongs[k].astype(BF16), wish, (((1,), (1,)), ((), ())), preferred_element_type=F32
        )
        slot = home[k : k + 1] * CAP + rank
        slot = jnp.where(owner[k : k + 1] == me.astype(F32), slots + local[k : k + 1], slot)
        slot = jnp.where(owner[k : k + 1] == twin.astype(F32), slots + cells + local[k : k + 1], slot)
        slot_rows[k : k + 1] = slot
    asks = asks.astype(jnp.int32)
    for q in range(half):
        req_out[q] = asks[2 * q : 2 * q + 2]

    valid = valid_ref[...].astype(F32)
    hour = (tm * hours + iota((hours, cells), 0)).astype(F32)
    mask = (hour < valid).astype(F32)
    mine = stats.at[tm]
    rural_in.wait()
    rural = rural_ref[...]
    mine[2:3] = jnp.sum(rural, axis=0, keepdims=True)
    mine[3:4] = jnp.sum(rural * rural, axis=0, keepdims=True)
    urban_in.wait()
    urban = urban_ref[...]
    mine[0:1] = jnp.sum(urban * mask, axis=0, keepdims=True)
    mine[1:2] = jnp.sum(urban * urban * mask, axis=0, keepdims=True)
    mine[4:8] = jnp.zeros((4, cells), F32)

    pl.semaphore_wait(barrier, half - 1 + 1 + nt - 1)

    @pl.loop(1, nt)
    def _(d):
        remote(STAT, stats.at[tm], stats.at[tm], tm=lax.rem(tm + d, nt)).start()


    @pl.loop(1, half)
    def _(d):
        other = lax.rem(place + d, half)
        remote(REQ, req_out.at[other], req_in.at[place], cells=side * half + other).start()

    req_in[place] = jnp.zeros((2, cells), jnp.int32)

    lane = iota((GROUP, cells), 1)
    row = iota((GROUP, cells), 0)
    lane_w = iota((wide, cells), 1)

    @pl.loop(0, groups, unroll=4)
    def _(g):
        one = lane == GROUP * g + row
        table = slot_rows[...]
        each = [jnp.where(one, table[k : k + 1], 0.0) for k in range(refs)]
        slot = jnp.sum(jnp.concatenate(each, axis=0), axis=1, keepdims=True).astype(jnp.int32)
        begin = pl.multiple_of(g * wide, wide)
        for j in range(slots // cells + 2):
            hit = slot == lane_w + j * cells
            pick[pl.ds(begin, wide), j * cells : (j + 1) * cells] = jnp.where(hit, 1.0, 0.0).astype(BF16)

    for p in range(PARTS):
        fetched[p, pl.ds(2 * place, 2)] = jnp.zeros((2, CAP, span), BF16)

    bytes_wait(stats.at[0 : nt - 1], rsem.at[STAT])
    total = stats[0]
    for i in range(1, nt):
        total += stats[i]

    def finish(series, first, second, n, keep):
        average = first / n
        spread = second / n - average * average
        return (series - average) * lax.rsqrt(spread + EPSILON) * keep

    rural_z = finish(rural_ref[...], total[2:3], total[3:4], F32(hours * nt), F32(1.0))
    for p in range(PARTS):
        turned = jnp.transpose(rural_z[p * span : (p + 1) * span]).astype(BF16)
        fetched[p, nc : nc + rows] = turned.reshape(rows, CAP, span)
        remote(
            TWIN + p, fetched.at[p, nc : nc + rows], fetched.at[p, nc + rows : nc + 2 * rows], cells=twin
        ).start()
    urban_z = finish(urban_ref[...], total[0:1], total[1:2], valid, mask)
    for j in range(hours // LAGS):
        ut[j] = jnp.transpose(urban_z[j * LAGS : (j + 1) * LAGS])
    halo_out[...] = ut[0].astype(BF16)

    @pl.when(tm > 0)
    def _():
        remote(HALO, halo_out, halo_in, tm=tm - 1).start()

    bytes_wait(req_in.at[0 : half - 1], rsem.at[REQ])
    batch = min(8, half)
    chunks = half // batch
    lane_c = iota((CAP, cells), 1)
    row_c = iota((CAP, cells), 0)
    here = lane_c == row_c
    height = batch * CAP
    lane_h = iota((height, cells), 1)

    def respond(rel, p, q):
        block = fetched[p, nc + rel * rows : nc + (rel + 1) * rows].reshape(cells, span)
        begin = pl.multiple_of(q * height, height)
        chosen = jnp.dot(choose[rel, pl.ds(begin, height), :], block, preferred_element_type=F32)
        answer[p, rel, pl.ds(q * batch, batch)] = chosen.astype(BF16).reshape(batch, CAP, span)

        @pl.loop(0, batch)
        def _(s):
            other = q * batch + s

            @pl.when(other != place)
            def _():
                remote(
                    FETCH + p, answer.at[p, rel, other], fetched.at[p, 2 * place + rel], cells=side * half + other
                ).start()

    def respond_all(rel, p):
        @pl.loop(0, chunks)
        def _(step):
            respond(rel, p, lax.rem(place // batch + step, chunks))

    @pl.loop(0, chunks)
    def _(step):
        q = lax.rem(place // batch + step, chunks)
        begin = pl.multiple_of(q * height, height)
        for rel in range(2):
            columns = []
            for s in range(batch):
                asked = req_in[q * batch + s][rel : rel + 1].astype(F32)
                columns.append(jnp.sum(jnp.where(here, asked, 0.0), axis=1, keepdims=True))
            column = jnp.concatenate(columns, axis=0).astype(jnp.int32)
            choose[rel, pl.ds(begin, height), :] = jnp.where(column == lane_h, 1.0, 0.0).astype(BF16)
        respond(0, 0, q)

    for p in range(1, PARTS):
        respond_all(0, p)

    @pl.when(tm < nt - 1)
    def _():
        bytes_wait(halo_in, rsem.at[HALO])
        ut[hours // LAGS] = halo_in[...].astype(F32)

    @pl.when(tm == nt - 1)
    def _():
        ut[hours // LAGS] = jnp.zeros((cells, LAGS), F32)

    tiles = hours // LAGS
    lane8 = iota((8, LAGS), 1)
    row8 = iota((8, LAGS), 0)

    def build(first, last):
        @pl.loop(first, last, unroll=8)
        def _(c):
            wave = [jnp.broadcast_to(ut[j, pl.ds(c, 1), :], (8, LAGS)) for j in range(tiles + 1)]
            for pair in range(share // 16):
                halves = []
                for a in (2 * pair, 2 * pair + 1):
                    shift = LAGS - share + 1 + 8 * a
                    turned = [pltpu.roll(x, shift, 1, stride=1, stride_axis=0) for x in wave]
                    turned.append(jnp.zeros((8, LAGS), F32))
                    upper = lane8 >= row8 + shift
                    halves.append([jnp.where(upper, turned[j + 1], turned[j]) for j in range(tiles + 1)])
                for j in range(tiles + 1):
                    both = jnp.concatenate([halves[0][j], halves[1][j]], axis=0).astype(BF16)
                    toep[c, 16 * pair : 16 * pair + 16, j * LAGS : (j + 1) * LAGS] = both

    step = cells // (2 * PARTS)
    for p in range(PARTS):
        build(p * step, (p + 1) * step)
        bytes_wait(fetched.at[p, nc + rows : nc + 2 * rows], rsem.at[TWIN + p])
        respond_all(1, p)

    build(cells // 2, cells)

    column_of = lax.rem(iota((share, nt * wide), 1), GROUP)
    lane_t = iota((4 * wide, LAGS), 1)
    lane_s = iota((share, 2 * wide), 1)
    reach = span + LAGS
    for p in range(PARTS):
        bytes_wait(fetched.at[p, 0 : nc - 2], rsem.at[FETCH + p])

        @pl.loop(0, quads)
        def _(quad):
            begin = pl.multiple_of(quad * 4 * wide, 4 * wide)
            chosen = jnp.dot(
                pick[pl.ds(begin, 4 * wide), :],
                fetched[p].reshape(slots + 2 * cells, span),
                preferred_element_type=F32,
            )
            pieces = [chosen[:, j * LAGS : (j + 1) * LAGS] for j in range(span // LAGS)]
            none = jnp.zeros((4 * wide, LAGS), F32)
            for a in range(nt):
                shift = share * a
                turned = [none] + [pltpu.roll(x, shift, 1) if a else x for x in pieces] + [none]
                for j in range(span // LAGS + 1):
                    piece = jnp.where(lane_t >= shift, turned[j + 1], turned[j]) if a else turned[j + 1]
                    piece = piece.astype(BF16)
                    for i in range(4):
                        moved[i, a, :, j * LAGS : (j + 1) * LAGS] = piece[i * wide : (i + 1) * wide]
            totals = []
            for i in range(4):
                g = 4 * quad + i
                left = toep[pl.ds(GROUP * g, GROUP), :, p * span : p * span + reach].reshape(GROUP * share, reach)
                sums = lax.dot_general(
                    left, moved[i].reshape(nt * wide, reach), (((1,), (1,)), ((), ())), preferred_element_type=F32
                )
                total = sums[0:share]
                for c in range(1, GROUP):
                    total = jnp.where(column_of == c, sums[c * share : (c + 1) * share], total)
                if p:
                    total += part[g]
                if p < PARTS - 1:
                    part[g] = total
                totals.append(total)
            if p == PARTS - 1:
                for h in range(2):
                    even, odd = totals[2 * h], totals[2 * h + 1]
                    blocks = []
                    for a in range(nt):
                        at = (a // 2) * 2 * wide
                        x, y = even[:, at : at + 2 * wide], odd[:, at : at + 2 * wide]
                        if a % 2:
                            x = pltpu.roll(x, wide, 1)
                        else:
                            y = pltpu.roll(y, wide, 1)
                        blocks.append(jnp.where(lane_s < wide, x, y))
                    peak = jnp.full((1, 2 * wide), 1e-30, F32)
                    for block in blocks:
                        peak = jnp.maximum(peak, jnp.max(jnp.abs(block), axis=0, keepdims=True))
                    peak_out[quad, h] = peak
                    scale = TOP / peak
                    for a in range(nt):
                        kept[quad, a, h] = blocks[a]
                        sums_out[quad, a, h] = (
                            jnp.floor(blocks[a] * scale + 0.5).astype(jnp.int32).astype(jnp.int16)
                        )

                @pl.loop(1, nt)
                def _(d):
                    peer = lax.rem(tm + d, nt)
                    remote(SUMS, sums_out.at[quad, peer], sums_in.at[tm, quad], tm=peer).start()
                    remote(PEAK, peak_out.at[quad], peak_in.at[tm, quad], tm=peer).start()

    sums_in[tm] = jnp.zeros((quads, 2, share, 2 * wide), jnp.int16)
    peak_in[tm] = jnp.zeros((quads, 2, 1, 2 * wide), F32)
    bytes_wait(sums_in.at[0 : nt - 1], rsem.at[SUMS])
    bytes_wait(peak_in.at[0 : nt - 1], rsem.at[PEAK])

    whole = []
    for quad in range(quads):
        for h in range(2):
            total = kept[quad, tm, h]
            for i in range(nt):
                total += sums_in[i, quad, h].astype(jnp.int32).astype(F32) * (peak_in[i, quad, h] * (1.0 / TOP))
            whole.append(total)
    lag = tm * share + (share - 1) - iota((share, cells), 0)
    overlap = (valid_ref[...] - lag).astype(F32)
    place_o = iota((share, cells), 1) // GROUP
    for k in range(refs):
        result = jnp.zeros((share, cells), F32)
        for g in range(groups):
            shift = (GROUP * g - wide * (g % 2) - GROUP * k) % cells
            piece = whole[g // 2]
            if shift:
                piece = pltpu.roll(piece, shift, 1)
            result = jnp.where(place_o == g, piece, result)
        result = result / overlap
        for i in range(share):
            out_ref[share - 1 - i, k : k + 1, :] = result[i : i + 1]

    bytes_wait(req_in.at[0 : half - 1], ssem.at[REQ])
    bytes_wait(stats.at[0 : nt - 1], ssem.at[STAT])

    @pl.when(tm > 0)
    def _():
        bytes_wait(halo_out, ssem.at[HALO])

    for p in range(PARTS):
        bytes_wait(fetched.at[p, nc : nc + rows], ssem.at[TWIN + p])
        bytes_wait(fetched.at[p, 0 : nc - 2], ssem.at[FETCH + p])
    bytes_wait(sums_in.at[0 : nt - 1], ssem.at[SUMS])
    bytes_wait(peak_in.at[0 : nt - 1], ssem.at[PEAK])


def solution(mesh):
    nc, nt = mesh.shape["cells"], mesh.shape["tm"]

    def shards(urban, rural, urban_valid, rural_ids):
        hours, cells = urban.shape
        refs = rural_ids.shape[0]
        share = LAGS // nt
        groups, wide, slots, half = cells // GROUP, GROUP * refs, nc * CAP, nc // 2
        quads = groups // 4
        span, rows = hours // PARTS, cells // CAP
        vmem = pl.BlockSpec(memory_space=pltpu.VMEM)
        whole = pl.BlockSpec(memory_space=pl.ANY)
        return pl.pallas_call(
            functools.partial(kernel, nc, nt),
            out_shape=jax.ShapeDtypeStruct((share, refs, cells), F32),
            in_specs=[whole, whole, vmem, vmem],
            out_specs=vmem,
            scratch_shapes=[
                pltpu.VMEM((hours, cells), F32),
                pltpu.VMEM((hours, cells), F32),
                pltpu.VMEM((half, 2, cells), jnp.int32),
                pltpu.VMEM((half, 2, cells), jnp.int32),
                pltpu.VMEM((refs, cells), F32),
                pltpu.VMEM((nt, 8, cells), F32),
                pltpu.VMEM((hours // LAGS + 1, cells, LAGS), F32),
                pltpu.VMEM((cells, LAGS), BF16),
                pltpu.VMEM((cells, LAGS), BF16),
                pltpu.VMEM((PARTS, 2, half, CAP, span), BF16),
                pltpu.VMEM((2, half * CAP, cells), BF16),
                pltpu.VMEM((PARTS, nc + 2 * rows, CAP, span), BF16),
                pltpu.VMEM((cells * refs, slots + 2 * cells), BF16),
                pltpu.VMEM((cells, share, hours + LAGS), BF16),
                pltpu.VMEM((4, nt, wide, span + LAGS), BF16),
                pltpu.VMEM((groups, share, nt * wide), F32),
                pltpu.VMEM((quads, nt, 2, share, 2 * wide), F32),
                pltpu.VMEM((quads, nt, 2, share, 2 * wide), jnp.int16),
                pltpu.VMEM((nt, quads, 2, share, 2 * wide), jnp.int16),
                pltpu.VMEM((quads, 2, 1, 2 * wide), F32),
                pltpu.VMEM((nt, quads, 2, 1, 2 * wide), F32),
                pltpu.SemaphoreType.DMA((2,)),
                pltpu.SemaphoreType.DMA((KINDS,)),
                pltpu.SemaphoreType.DMA((KINDS,)),
            ],
            compiler_params=pltpu.CompilerParams(
                collective_id=0, has_side_effects=True, vmem_limit_bytes=52 * 1024 * 1024
            ),
        )(urban, rural, urban_valid.reshape(1, cells), rural_ids)

    in_specs = (P("tm", "cells"), P("tm", "cells"), P("cells"), P(None, "cells"))
    return jax.shard_map(
        shards, mesh=mesh, in_specs=in_specs, out_specs=P("tm", None, "cells"), check_vma=False
    )
```

```python
import functools

import jax
import jax.numpy as jnp
from jax import lax
from jax.experimental import pallas as pl
from jax.experimental.pallas import tpu as pltpu
from jax.sharding import PartitionSpec as P

LAGS = 128
EPSILON = 1e-05
CAP = 16
GROUP = 8
PARTS = 2
MESH = pl.DeviceIdType.MESH
F32 = jnp.float32
BF16 = jnp.bfloat16

REQ, STAT, HALO, SUMS, PEAK, TWIN, FETCH = 0, 1, 2, 3, 4, 5, 5 + PARTS
KINDS = 5 + 2 * PARTS
TOP = 32760.0


def iota(shape, axis):
    return lax.broadcasted_iota(jnp.int32, shape, axis)


def bytes_wait(ref, sem):
    pltpu.make_async_copy(ref, ref, sem).wait()


def kernel(
    nc, nt, urban_hbm, rural_hbm, valid_ref, ids_ref, out_ref,
    urban_ref, rural_ref, req_out, req_in, slot_rows, stats, ut, halo_out, halo_in,
    answer, choose, fetched, pick, toep, moved, part, kept, sums_out, sums_in, peak_out, peak_in, local_sem, ssem, rsem,
):
    hours, cells = urban_ref.shape
    refs = ids_ref.shape[0]
    share = LAGS // nt
    groups = cells // GROUP
    wide = GROUP * refs
    quads = groups // 4
    slots = nc * CAP
    half = nc // 2
    rows = cells // CAP
    span = hours // PARTS
    me = lax.axis_index("cells")
    tm = lax.axis_index("tm")
    side = me // half
    place = lax.rem(me, half)
    twin = (1 - side) * half + place

    def remote(kind, src, dst, **where):
        return pltpu.make_async_remote_copy(
            src_ref=src, dst_ref=dst, send_sem=ssem.at[kind], recv_sem=rsem.at[kind],
            device_id=where, device_id_type=MESH,
        )

    barrier = pltpu.get_barrier_semaphore()

    @pl.loop(1, nt)
    def _(d):
        pl.semaphore_signal(barrier, inc=1, device_id={"tm": lax.rem(tm + d, nt)}, device_id_type=MESH)

    pl.semaphore_signal(barrier, inc=1, device_id={"cells": twin}, device_id_type=MESH)

    @pl.loop(1, half)
    def _(d):
        peer = side * half + lax.rem(place + d, half)
        pl.semaphore_signal(barrier, inc=1, device_id={"cells": peer}, device_id_type=MESH)

    rural_in = pltpu.make_async_copy(rural_hbm, rural_ref, local_sem.at[0])
    urban_in = pltpu.make_async_copy(urban_hbm, urban_ref, local_sem.at[1])
    rural_in.start()
    urban_in.start()

    ids = ids_ref[...]
    owner = (ids >> 7).astype(F32)
    local = (ids & 127).astype(F32)
    upper = jnp.where(owner >= half, 1.0, 0.0)
    away = jnp.where(upper == side.astype(F32), 0.0, 1.0)
    home = (owner - half * upper) * 2.0 + away
    home_i = iota((nc, cells), 0).astype(F32)
    belongs = [jnp.where(home[k : k + 1] == home_i, 1.0, 0.0) for k in range(refs)]
    earlier = iota((cells, 2 * cells), 0) < iota((cells, 2 * cells), 1)
    counts = jnp.dot(
        jnp.concatenate(belongs, axis=0).astype(BF16), jnp.where(earlier, 1.0, 0.0).astype(BF16),
        preferred_element_type=F32,
    )
    before = jnp.zeros((nc, cells), F32)
    rank_i = iota((cells, cells), 0).astype(F32)
    asks = jnp.zeros((nc, cells), F32)
    for k in range(refs):
        count = counts[k * nc : (k + 1) * nc]
        rank = jnp.sum(belongs[k] * (count[:, 0:cells] + before), axis=0, keepdims=True)
        before += count[:, cells : 2 * cells]
        wish = jnp.where(rank == rank_i, local[k : k + 1], 0.0).astype(BF16)
        asks += lax.dot_general(
            belongs[k].astype(BF16), wish, (((1,), (1,)), ((), ())), preferred_element_type=F32
        )
        slot = home[k : k + 1] * CAP + rank
        slot = jnp.where(owner[k : k + 1] == me.astype(F32), slots + local[k : k + 1], slot)
        slot = jnp.where(owner[k : k + 1] == twin.astype(F32), slots + cells + local[k : k + 1], slot)
        slot_rows[k : k + 1] = slot
    asks = asks.astype(jnp.int32)
    for q in range(half):
        req_out[q] = asks[2 * q : 2 * q + 2]

    valid = valid_ref[...].astype(F32)
    hour = (tm * hours + iota((hours, cells), 0)).astype(F32)
    mask = (hour < valid).astype(F32)
    mine = stats.at[tm]
    rural_in.wait()
    rural = rural_ref[...]
    mine[2:3] = jnp.sum(rural, axis=0, keepdims=True)
    mine[3:4] = jnp.sum(rural * rural, axis=0, keepdims=True)
    urban_in.wait()
    urban = urban_ref[...]
    mine[0:1] = jnp.sum(urban * mask, axis=0, keepdims=True)
    mine[1:2] = jnp.sum(urban * urban * mask, axis=0, keepdims=True)
    mine[4:8] = jnp.zeros((4, cells), F32)

    pl.semaphore_wait(barrier, half - 1 + 1 + nt - 1)

    @pl.loop(1, nt)
    def _(d):
        remote(STAT, stats.at[tm], stats.at[tm], tm=lax.rem(tm + d, nt)).start()


    @pl.loop(1, half)
    def _(d):
        other = lax.rem(place + d, half)
        remote(REQ, req_out.at[other], req_in.at[place], cells=side * half + other).start()

    req_in[place] = jnp.zeros((2, cells), jnp.int32)

    lane = iota((GROUP, cells), 1)
    row = iota((GROUP, cells), 0)
    lane_w = iota((wide, cells), 1)

    @pl.loop(0, groups, unroll=4)
    def _(g):
        one = lane == GROUP * g + row
        table = slot_rows[...]
        each = [jnp.where(one, table[k : k + 1], 0.0) for k in range(refs)]
        slot = jnp.sum(jnp.concatenate(each, axis=0), axis=1, keepdims=True).astype(jnp.int32)
        begin = pl.multiple_of(g * wide, wide)
        for j in range(slots // cells + 2):
            hit = slot == lane_w + j * cells
            pick[pl.ds(begin, wide), j * cells : (j + 1) * cells] = jnp.where(hit, 1.0, 0.0).astype(BF16)

    for p in range(PARTS):
        fetched[p, pl.ds(2 * place, 2)] = jnp.zeros((2, CAP, span), BF16)

    bytes_wait(stats.at[0 : nt - 1], rsem.at[STAT])
    total = stats[0]
    for i in range(1, nt):
        total += stats[i]

    def finish(series, first, second, n, keep):
        average = first / n
        spread = second / n - average * average
        return (series - average) * lax.rsqrt(spread + EPSILON) * keep

    for p in range(PARTS):
        rural_z = finish(rural_ref[p * span : (p + 1) * span], total[2:3], total[3:4], F32(hours * nt), F32(1.0))
        turned = jnp.transpose(rural_z).astype(BF16)
        fetched[p, nc : nc + rows] = turned.reshape(rows, CAP, span)
        remote(
            TWIN + p, fetched.at[p, nc : nc + rows], fetched.at[p, nc + rows : nc + 2 * rows], cells=twin
        ).start()
    bytes_wait(req_in.at[0 : half - 1], rsem.at[REQ])
    batch = min(8, half)
    chunks = half // batch
    lane_c = iota((CAP, cells), 1)
    row_c = iota((CAP, cells), 0)
    here = lane_c == row_c
    height = batch * CAP
    lane_h = iota((height, cells), 1)

    def respond(rel, p, q):
        block = fetched[p, nc + rel * rows : nc + (rel + 1) * rows].reshape(cells, span)
        begin = pl.multiple_of(q * height, height)
        chosen = jnp.dot(choose[rel, pl.ds(begin, height), :], block, preferred_element_type=F32)
        answer[p, rel, pl.ds(q * batch, batch)] = chosen.astype(BF16).reshape(batch, CAP, span)

        @pl.loop(0, batch)
        def _(s):
            other = q * batch + s

            @pl.when(other != place)
            def _():
                remote(
                    FETCH + p, answer.at[p, rel, other], fetched.at[p, 2 * place + rel], cells=side * half + other
                ).start()

    def respond_all(rel, p):
        @pl.loop(0, chunks)
        def _(step):
            respond(rel, p, lax.rem(place // batch + step, chunks))

    @pl.loop(0, chunks)
    def _(step):
        q = lax.rem(place // batch + step, chunks)
        begin = pl.multiple_of(q * height, height)
        for rel in range(2):
            columns = []
            for s in range(batch):
                asked = req_in[q * batch + s][rel : rel + 1].astype(F32)
                columns.append(jnp.sum(jnp.where(here, asked, 0.0), axis=1, keepdims=True))
            column = jnp.concatenate(columns, axis=0).astype(jnp.int32)
            choose[rel, pl.ds(begin, height), :] = jnp.where(column == lane_h, 1.0, 0.0).astype(BF16)
        respond(0, 0, q)

    urban_z = finish(urban_ref[...], total[0:1], total[1:2], valid, mask)
    for j in range(hours // LAGS):
        ut[j] = jnp.transpose(urban_z[j * LAGS : (j + 1) * LAGS])
    halo_out[...] = ut[0].astype(BF16)

    @pl.when(tm > 0)
    def _():
        remote(HALO, halo_out, halo_in, tm=tm - 1).start()

    tiles = hours // LAGS
    lane8 = iota((8, LAGS), 1)
    row8 = iota((8, LAGS), 0)

    def build(first, last):
        @pl.loop(first, last, unroll=8)
        def _(c):
            wave = [jnp.broadcast_to(ut[j, pl.ds(c, 1), :], (8, LAGS)) for j in range(tiles + 1)]
            for pair in range(share // 16):
                halves = []
                for a in (2 * pair, 2 * pair + 1):
                    shift = LAGS - share + 1 + 8 * a
                    turned = [pltpu.roll(x, shift, 1, stride=1, stride_axis=0) for x in wave]
                    turned.append(jnp.zeros((8, LAGS), F32))
                    upper = lane8 >= row8 + shift
                    halves.append([jnp.where(upper, turned[j + 1], turned[j]) for j in range(tiles + 1)])
                for j in range(tiles + 1):
                    both = jnp.concatenate([halves[0][j], halves[1][j]], axis=0).astype(BF16)
                    toep[c, 16 * pair : 16 * pair + 16, j * LAGS : (j + 1) * LAGS] = both

    bytes_wait(fetched.at[0, nc + rows : nc + 2 * rows], rsem.at[TWIN + 0])
    respond_all(1, 0)
    respond_all(0, 1)
    bytes_wait(fetched.at[1, nc + rows : nc + 2 * rows], rsem.at[TWIN + 1])
    respond_all(1, 1)
    @pl.when(tm < nt - 1)
    def _():
        bytes_wait(halo_in, rsem.at[HALO])
        ut[hours // LAGS] = halo_in[...].astype(F32)

    @pl.when(tm == nt - 1)
    def _():
        ut[hours // LAGS] = jnp.zeros((cells, LAGS), F32)

    build(0, cells)
    column_of = lax.rem(iota((share, nt * wide), 1), GROUP)
    lane_t = iota((4 * wide, LAGS), 1)
    lane_s = iota((share, 2 * wide), 1)
    reach = span + LAGS
    for p in range(PARTS):
        bytes_wait(fetched.at[p, 0 : nc - 2], rsem.at[FETCH + p])

        @pl.loop(0, quads)
        def _(quad):
            begin = pl.multiple_of(quad * 4 * wide, 4 * wide)
            chosen = jnp.dot(
                pick[pl.ds(begin, 4 * wide), :],
                fetched[p].reshape(slots + 2 * cells, span),
                preferred_element_type=F32,
            )
            pieces = [chosen[:, j * LAGS : (j + 1) * LAGS] for j in range(span // LAGS)]
            none = jnp.zeros((4 * wide, LAGS), F32)
            for a in range(nt):
                shift = share * a
                turned = [none] + [pltpu.roll(x, shift, 1) if a else x for x in pieces] + [none]
                for j in range(span // LAGS + 1):
                    piece = jnp.where(lane_t >= shift, turned[j + 1], turned[j]) if a else turned[j + 1]
                    piece = piece.astype(BF16)
                    for i in range(4):
                        moved[i, a, :, j * LAGS : (j + 1) * LAGS] = piece[i * wide : (i + 1) * wide]
            totals = []
            for i in range(4):
                g = 4 * quad + i
                left = toep[pl.ds(GROUP * g, GROUP), :, p * span : p * span + reach].reshape(GROUP * share, reach)
                sums = lax.dot_general(
                    left, moved[i].reshape(nt * wide, reach), (((1,), (1,)), ((), ())), preferred_element_type=F32
                )
                total = sums[0:share]
                for c in range(1, GROUP):
                    total = jnp.where(column_of == c, sums[c * share : (c + 1) * share], total)
                if p:
                    total += part[g]
                if p < PARTS - 1:
                    part[g] = total
                totals.append(total)
            if p == PARTS - 1:
                for h in range(2):
                    even, odd = totals[2 * h], totals[2 * h + 1]
                    blocks = []
                    for a in range(nt):
                        at = (a // 2) * 2 * wide
                        x, y = even[:, at : at + 2 * wide], odd[:, at : at + 2 * wide]
                        if a % 2:
                            x = pltpu.roll(x, wide, 1)
                        else:
                            y = pltpu.roll(y, wide, 1)
                        blocks.append(jnp.where(lane_s < wide, x, y))
                    peak = jnp.full((1, 2 * wide), 1e-30, F32)
                    for block in blocks:
                        peak = jnp.maximum(peak, jnp.max(jnp.abs(block), axis=0, keepdims=True))
                    peak_out[quad, h] = peak
                    scale = TOP / peak
                    for a in range(nt):
                        kept[quad, a, h] = blocks[a]
                        sums_out[quad, a, h] = (
                            jnp.floor(blocks[a] * scale + 0.5).astype(jnp.int32).astype(jnp.int16)
                        )

                @pl.loop(1, nt)
                def _(d):
                    peer = lax.rem(tm + d, nt)
                    remote(SUMS, sums_out.at[quad, peer], sums_in.at[tm, quad], tm=peer).start()
                    remote(PEAK, peak_out.at[quad], peak_in.at[tm, quad], tm=peer).start()

    sums_in[tm] = jnp.zeros((quads, 2, share, 2 * wide), jnp.int16)
    peak_in[tm] = jnp.zeros((quads, 2, 1, 2 * wide), F32)
    bytes_wait(sums_in.at[0 : nt - 1], rsem.at[SUMS])
    bytes_wait(peak_in.at[0 : nt - 1], rsem.at[PEAK])

    whole = []
    for quad in range(quads):
        for h in range(2):
            total = kept[quad, tm, h]
            for i in range(nt):
                total += sums_in[i, quad, h].astype(jnp.int32).astype(F32) * (peak_in[i, quad, h] * (1.0 / TOP))
            whole.append(total)
    lag = tm * share + (share - 1) - iota((share, cells), 0)
    overlap = (valid_ref[...] - lag).astype(F32)
    place_o = iota((share, cells), 1) // GROUP
    for k in range(refs):
        result = jnp.zeros((share, cells), F32)
        for g in range(groups):
            shift = (GROUP * g - wide * (g % 2) - GROUP * k) % cells
            piece = whole[g // 2]
            if shift:
                piece = pltpu.roll(piece, shift, 1)
            result = jnp.where(place_o == g, piece, result)
        result = result / overlap
        for i in range(share):
            out_ref[share - 1 - i, k : k + 1, :] = result[i : i + 1]

    bytes_wait(req_in.at[0 : half - 1], ssem.at[REQ])
    bytes_wait(stats.at[0 : nt - 1], ssem.at[STAT])

    @pl.when(tm > 0)
    def _():
        bytes_wait(halo_out, ssem.at[HALO])

    for p in range(PARTS):
        bytes_wait(fetched.at[p, nc : nc + rows], ssem.at[TWIN + p])
        bytes_wait(fetched.at[p, 0 : nc - 2], ssem.at[FETCH + p])
    bytes_wait(sums_in.at[0 : nt - 1], ssem.at[SUMS])
    bytes_wait(peak_in.at[0 : nt - 1], ssem.at[PEAK])


def solution(mesh):
    nc, nt = mesh.shape["cells"], mesh.shape["tm"]

    def shards(urban, rural, urban_valid, rural_ids):
        hours, cells = urban.shape
        refs = rural_ids.shape[0]
        share = LAGS // nt
        groups, wide, slots, half = cells // GROUP, GROUP * refs, nc * CAP, nc // 2
        quads = groups // 4
        span, rows = hours // PARTS, cells // CAP
        vmem = pl.BlockSpec(memory_space=pltpu.VMEM)
        whole = pl.BlockSpec(memory_space=pl.ANY)
        return pl.pallas_call(
            functools.partial(kernel, nc, nt),
            out_shape=jax.ShapeDtypeStruct((share, refs, cells), F32),
            in_specs=[whole, whole, vmem, vmem],
            out_specs=vmem,
            scratch_shapes=[
                pltpu.VMEM((hours, cells), F32),
                pltpu.VMEM((hours, cells), F32),
                pltpu.VMEM((half, 2, cells), jnp.int32),
                pltpu.VMEM((half, 2, cells), jnp.int32),
                pltpu.VMEM((refs, cells), F32),
                pltpu.VMEM((nt, 8, cells), F32),
                pltpu.VMEM((hours // LAGS + 1, cells, LAGS), F32),
                pltpu.VMEM((cells, LAGS), BF16),
                pltpu.VMEM((cells, LAGS), BF16),
                pltpu.VMEM((PARTS, 2, half, CAP, span), BF16),
                pltpu.VMEM((2, half * CAP, cells), BF16),
                pltpu.VMEM((PARTS, nc + 2 * rows, CAP, span), BF16),
                pltpu.VMEM((cells * refs, slots + 2 * cells), BF16),
                pltpu.VMEM((cells, share, hours + LAGS), BF16),
                pltpu.VMEM((4, nt, wide, span + LAGS), BF16),
                pltpu.VMEM((groups, share, nt * wide), F32),
                pltpu.VMEM((quads, nt, 2, share, 2 * wide), F32),
                pltpu.VMEM((quads, nt, 2, share, 2 * wide), jnp.int16),
                pltpu.VMEM((nt, quads, 2, share, 2 * wide), jnp.int16),
                pltpu.VMEM((quads, 2, 1, 2 * wide), F32),
                pltpu.VMEM((nt, quads, 2, 1, 2 * wide), F32),
                pltpu.SemaphoreType.DMA((2,)),
                pltpu.SemaphoreType.DMA((KINDS,)),
                pltpu.SemaphoreType.DMA((KINDS,)),
            ],
            compiler_params=pltpu.CompilerParams(
                collective_id=0, has_side_effects=True, vmem_limit_bytes=52 * 1024 * 1024
            ),
        )(urban, rural, urban_valid.reshape(1, cells), rural_ids)

    in_specs = (P("tm", "cells"), P("tm", "cells"), P("cells"), P(None, "cells"))
    return jax.shard_map(
        shards, mesh=mesh, in_specs=in_specs, out_specs=P("tm", None, "cells"), check_vma=False
    )
```

```python
import functools

import jax
import jax.numpy as jnp
from jax import lax
from jax.experimental import pallas as pl
from jax.experimental.pallas import tpu as pltpu
from jax.sharding import PartitionSpec as P

LAGS = 128
EPSILON = 1e-05
CAP = 16
GROUP = 8
PARTS = 2
MESH = pl.DeviceIdType.MESH
F32 = jnp.float32
BF16 = jnp.bfloat16

REQ, STAT, HALO, SUMS, PEAK, TWIN, FETCH = 0, 1, 2, 3, 4, 5, 5 + PARTS
KINDS = 5 + 2 * PARTS
TOP = 32760.0


def iota(shape, axis):
    return lax.broadcasted_iota(jnp.int32, shape, axis)


def bytes_wait(ref, sem):
    pltpu.make_async_copy(ref, ref, sem).wait()


def kernel(
    nc, nt, urban_hbm, rural_hbm, valid_ref, ids_ref, out_ref,
    urban_ref, rural_ref, req_out, req_in, slot_rows, stats, ut, halo_out, halo_in,
    answer, choose, fetched, pick, toep, moved, part, kept, sums_out, sums_in, peak_out, peak_in, local_sem, ssem, rsem,
):
    hours, cells = urban_ref.shape
    refs = ids_ref.shape[0]
    share = LAGS // nt
    groups = cells // GROUP
    wide = GROUP * refs
    quads = groups // 4
    slots = nc * CAP
    half = nc // 2
    rows = cells // CAP
    span = hours // PARTS
    me = lax.axis_index("cells")
    tm = lax.axis_index("tm")
    side = me // half
    place = lax.rem(me, half)
    twin = (1 - side) * half + place

    def remote(kind, src, dst, **where):
        return pltpu.make_async_remote_copy(
            src_ref=src, dst_ref=dst, send_sem=ssem.at[kind], recv_sem=rsem.at[kind],
            device_id=where, device_id_type=MESH,
        )

    barrier = pltpu.get_barrier_semaphore()

    @pl.loop(1, nt)
    def _(d):
        pl.semaphore_signal(barrier, inc=1, device_id={"tm": lax.rem(tm + d, nt)}, device_id_type=MESH)

    pl.semaphore_signal(barrier, inc=1, device_id={"cells": twin}, device_id_type=MESH)

    @pl.loop(1, half)
    def _(d):
        peer = side * half + lax.rem(place + d, half)
        pl.semaphore_signal(barrier, inc=1, device_id={"cells": peer}, device_id_type=MESH)

    rural_in = pltpu.make_async_copy(rural_hbm, rural_ref, local_sem.at[0])
    urban_in = pltpu.make_async_copy(urban_hbm, urban_ref, local_sem.at[1])
    rural_in.start()
    urban_in.start()

    ids = ids_ref[...]
    owner = (ids >> 7).astype(F32)
    local = (ids & 127).astype(F32)
    upper = jnp.where(owner >= half, 1.0, 0.0)
    away = jnp.where(upper == side.astype(F32), 0.0, 1.0)
    home = (owner - half * upper) * 2.0 + away
    home_i = iota((nc, cells), 0).astype(F32)
    belongs = [jnp.where(home[k : k + 1] == home_i, 1.0, 0.0) for k in range(refs)]
    earlier = iota((cells, 2 * cells), 0) < iota((cells, 2 * cells), 1)
    counts = jnp.dot(
        jnp.concatenate(belongs, axis=0).astype(BF16), jnp.where(earlier, 1.0, 0.0).astype(BF16),
        preferred_element_type=F32,
    )
    before = jnp.zeros((nc, cells), F32)
    rank_i = iota((cells, cells), 0).astype(F32)
    asks = jnp.zeros((nc, cells), F32)
    for k in range(refs):
        count = counts[k * nc : (k + 1) * nc]
        rank = jnp.sum(belongs[k] * (count[:, 0:cells] + before), axis=0, keepdims=True)
        before += count[:, cells : 2 * cells]
        wish = jnp.where(rank == rank_i, local[k : k + 1], 0.0).astype(BF16)
        asks += lax.dot_general(
            belongs[k].astype(BF16), wish, (((1,), (1,)), ((), ())), preferred_element_type=F32
        )
        slot = home[k : k + 1] * CAP + rank
        slot = jnp.where(owner[k : k + 1] == me.astype(F32), slots + local[k : k + 1], slot)
        slot = jnp.where(owner[k : k + 1] == twin.astype(F32), slots + cells + local[k : k + 1], slot)
        slot_rows[k : k + 1] = slot
    asks = asks.astype(jnp.int32)
    for q in range(half):
        req_out[q] = asks[2 * q : 2 * q + 2]

    valid = valid_ref[...].astype(F32)
    hour = (tm * hours + iota((hours, cells), 0)).astype(F32)
    mask = (hour < valid).astype(F32)
    mine = stats.at[tm]
    rural_in.wait()
    rural = rural_ref[...]
    mine[2:3] = jnp.sum(rural, axis=0, keepdims=True)
    mine[3:4] = jnp.sum(rural * rural, axis=0, keepdims=True)
    urban_in.wait()
    urban = urban_ref[...]
    mine[0:1] = jnp.sum(urban * mask, axis=0, keepdims=True)
    mine[1:2] = jnp.sum(urban * urban * mask, axis=0, keepdims=True)
    mine[4:8] = jnp.zeros((4, cells), F32)

    pl.semaphore_wait(barrier, half - 1 + 1 + nt - 1)

    @pl.loop(1, nt)
    def _(d):
        remote(STAT, stats.at[tm], stats.at[tm], tm=lax.rem(tm + d, nt)).start()


    @pl.loop(1, half)
    def _(d):
        other = lax.rem(place + d, half)
        remote(REQ, req_out.at[other], req_in.at[place], cells=side * half + other).start()

    req_in[place] = jnp.zeros((2, cells), jnp.int32)

    lane = iota((GROUP, cells), 1)
    row = iota((GROUP, cells), 0)
    lane_w = iota((wide, cells), 1)

    @pl.loop(0, groups, unroll=4)
    def _(g):
        one = lane == GROUP * g + row
        table = slot_rows[...]
        each = [jnp.where(one, table[k : k + 1], 0.0) for k in range(refs)]
        slot = jnp.sum(jnp.concatenate(each, axis=0), axis=1, keepdims=True).astype(jnp.int32)
        begin = pl.multiple_of(g * wide, wide)
        for j in range(slots // cells + 2):
            hit = slot == lane_w + j * cells
            pick[pl.ds(begin, wide), j * cells : (j + 1) * cells] = jnp.where(hit, 1.0, 0.0).astype(BF16)

    for p in range(PARTS):
        fetched[p, pl.ds(2 * place, 2)] = jnp.zeros((2, CAP, span), BF16)

    bytes_wait(stats.at[0 : nt - 1], rsem.at[STAT])
    total = stats[0]
    for i in range(1, nt):
        total += stats[i]

    def finish(series, first, second, n, keep):
        average = first / n
        spread = second / n - average * average
        return (series - average) * lax.rsqrt(spread + EPSILON) * keep

    for p in range(PARTS):
        rural_z = finish(rural_ref[p * span : (p + 1) * span], total[2:3], total[3:4], F32(hours * nt), F32(1.0))
        turned = jnp.transpose(rural_z).astype(BF16)
        fetched[p, nc : nc + rows] = turned.reshape(rows, CAP, span)
        remote(
            TWIN + p, fetched.at[p, nc : nc + rows], fetched.at[p, nc + rows : nc + 2 * rows], cells=twin
        ).start()
    bytes_wait(req_in.at[0 : half - 1], rsem.at[REQ])
    batch = min(8, half)
    chunks = half // batch
    lane_c = iota((CAP, cells), 1)
    row_c = iota((CAP, cells), 0)
    here = lane_c == row_c
    height = batch * CAP
    lane_h = iota((height, cells), 1)

    def respond(rel, p, q):
        block = fetched[p, nc + rel * rows : nc + (rel + 1) * rows].reshape(cells, span)
        begin = pl.multiple_of(q * height, height)
        chosen = jnp.dot(choose[rel, pl.ds(begin, height), :], block, preferred_element_type=F32)
        answer[p, rel, pl.ds(q * batch, batch)] = chosen.astype(BF16).reshape(batch, CAP, span)

        @pl.loop(0, batch)
        def _(s):
            other = q * batch + s

            @pl.when(other != place)
            def _():
                remote(
                    FETCH + p, answer.at[p, rel, other], fetched.at[p, 2 * place + rel], cells=side * half + other
                ).start()

    def respond_all(rel, p):
        @pl.loop(0, chunks)
        def _(step):
            respond(rel, p, lax.rem(place // batch + step, chunks))

    @pl.loop(0, chunks)
    def _(step):
        q = lax.rem(place // batch + step, chunks)
        begin = pl.multiple_of(q * height, height)
        for rel in range(2):
            columns = []
            for s in range(batch):
                asked = req_in[q * batch + s][rel : rel + 1].astype(F32)
                columns.append(jnp.sum(jnp.where(here, asked, 0.0), axis=1, keepdims=True))
            column = jnp.concatenate(columns, axis=0).astype(jnp.int32)
            choose[rel, pl.ds(begin, height), :] = jnp.where(column == lane_h, 1.0, 0.0).astype(BF16)
        respond(0, 0, q)

    urban_z = finish(urban_ref[...], total[0:1], total[1:2], valid, mask)
    for j in range(hours // LAGS):
        ut[j] = jnp.transpose(urban_z[j * LAGS : (j + 1) * LAGS])
    halo_out[...] = ut[0].astype(BF16)

    @pl.when(tm > 0)
    def _():
        remote(HALO, halo_out, halo_in, tm=tm - 1).start()

    tiles = hours // LAGS
    lane8 = iota((8, LAGS), 1)
    row8 = iota((8, LAGS), 0)

    def build(first, last):
        @pl.loop(first, last, unroll=8)
        def _(c):
            wave = [jnp.broadcast_to(ut[j, pl.ds(c, 1), :], (8, LAGS)) for j in range(tiles + 1)]
            for pair in range(share // 16):
                halves = []
                for a in (2 * pair, 2 * pair + 1):
                    shift = LAGS - share + 1 + 8 * a
                    turned = [pltpu.roll(x, shift, 1, stride=1, stride_axis=0) for x in wave]
                    turned.append(jnp.zeros((8, LAGS), F32))
                    upper = lane8 >= row8 + shift
                    halves.append([jnp.where(upper, turned[j + 1], turned[j]) for j in range(tiles + 1)])
                for j in range(tiles + 1):
                    both = jnp.concatenate([halves[0][j], halves[1][j]], axis=0).astype(BF16)
                    toep[c, 16 * pair : 16 * pair + 16, j * LAGS : (j + 1) * LAGS] = both

    bytes_wait(fetched.at[0, nc + rows : nc + 2 * rows], rsem.at[TWIN + 0])
    respond_all(1, 0)
    respond_all(0, 1)
    bytes_wait(fetched.at[1, nc + rows : nc + 2 * rows], rsem.at[TWIN + 1])
    respond_all(1, 1)
    @pl.when(tm < nt - 1)
    def _():
        bytes_wait(halo_in, rsem.at[HALO])
        ut[hours // LAGS] = halo_in[...].astype(F32)

    @pl.when(tm == nt - 1)
    def _():
        ut[hours // LAGS] = jnp.zeros((cells, LAGS), F32)

    build(0, cells)
    column_of = lax.rem(iota((share, nt * wide), 1), GROUP)
    lane_t = iota((4 * wide, LAGS), 1)
    lane_s = iota((share, 2 * wide), 1)
    reach = span + LAGS
    for p in range(PARTS):
        bytes_wait(fetched.at[p, 0 : nc - 2], rsem.at[FETCH + p])

        for lot in ([range(quads)] if p < PARTS - 1 else [range(0, 2), range(2, quads)]):
            for quad in lot:
                begin = quad * 4 * wide
                chosen = jnp.dot(
                    pick[begin : begin + 4 * wide, :],
                    fetched[p].reshape(slots + 2 * cells, span),
                    preferred_element_type=F32,
                )
                pieces = [chosen[:, j * LAGS : (j + 1) * LAGS] for j in range(span // LAGS)]
                none = jnp.zeros((4 * wide, LAGS), F32)
                for a in range(nt):
                    shift = share * a
                    turned = [none] + [pltpu.roll(x, shift, 1) if a else x for x in pieces] + [none]
                    for j in range(span // LAGS + 1):
                        piece = jnp.where(lane_t >= shift, turned[j + 1], turned[j]) if a else turned[j + 1]
                        piece = piece.astype(BF16)
                        for i in range(4):
                            moved[quad, i, a, :, j * LAGS : (j + 1) * LAGS] = piece[i * wide : (i + 1) * wide]
            for quad in lot:
                totals = []
                for i in range(4):
                    g = 4 * quad + i
                    left = toep[GROUP * g : GROUP * (g + 1), :, p * span : p * span + reach].reshape(GROUP * share, reach)
                    sums = lax.dot_general(
                        left, moved[quad, i].reshape(nt * wide, reach), (((1,), (1,)), ((), ())), preferred_element_type=F32
                    )
                    total = sums[0:share]
                    for c in range(1, GROUP):
                        total = jnp.where(column_of == c, sums[c * share : (c + 1) * share], total)
                    if p:
                        total += part[g]
                    if p < PARTS - 1:
                        part[g] = total
                    totals.append(total)
                if p == PARTS - 1:
                    for h in range(2):
                        even, odd = totals[2 * h], totals[2 * h + 1]
                        blocks = []
                        for a in range(nt):
                            at = (a // 2) * 2 * wide
                            x, y = even[:, at : at + 2 * wide], odd[:, at : at + 2 * wide]
                            if a % 2:
                                x = pltpu.roll(x, wide, 1)
                            else:
                                y = pltpu.roll(y, wide, 1)
                            blocks.append(jnp.where(lane_s < wide, x, y))
                        peak = jnp.full((1, 2 * wide), 1e-30, F32)
                        for block in blocks:
                            peak = jnp.maximum(peak, jnp.max(jnp.abs(block), axis=0, keepdims=True))
                        peak_out[quad, h] = peak
                        scale = TOP / peak
                        for a in range(nt):
                            kept[quad, a, h] = blocks[a]
                            sums_out[quad, a, h] = (
                                jnp.floor(blocks[a] * scale + 0.5).astype(jnp.int32).astype(jnp.int16)
                            )

                    for d in range(1, nt):
                        peer = lax.rem(tm + d, nt)
                        remote(SUMS, sums_out.at[quad, peer], sums_in.at[tm, quad], tm=peer).start()
                        remote(PEAK, peak_out.at[quad], peak_in.at[tm, quad], tm=peer).start()

    sums_in[tm] = jnp.zeros((quads, 2, share, 2 * wide), jnp.int16)
    peak_in[tm] = jnp.zeros((quads, 2, 1, 2 * wide), F32)
    bytes_wait(sums_in.at[0 : nt - 1], rsem.at[SUMS])
    bytes_wait(peak_in.at[0 : nt - 1], rsem.at[PEAK])

    whole = []
    for quad in range(quads):
        for h in range(2):
            total = kept[quad, tm, h]
            for i in range(nt):
                total += sums_in[i, quad, h].astype(jnp.int32).astype(F32) * (peak_in[i, quad, h] * (1.0 / TOP))
            whole.append(total)
    lag = tm * share + (share - 1) - iota((share, cells), 0)
    overlap = (valid_ref[...] - lag).astype(F32)
    place_o = iota((share, cells), 1) // GROUP
    for k in range(refs):
        result = jnp.zeros((share, cells), F32)
        for g in range(groups):
            shift = (GROUP * g - wide * (g % 2) - GROUP * k) % cells
            piece = whole[g // 2]
            if shift:
                piece = pltpu.roll(piece, shift, 1)
            result = jnp.where(place_o == g, piece, result)
        result = result / overlap
        for i in range(share):
            out_ref[share - 1 - i, k : k + 1, :] = result[i : i + 1]

    bytes_wait(req_in.at[0 : half - 1], ssem.at[REQ])
    bytes_wait(stats.at[0 : nt - 1], ssem.at[STAT])

    @pl.when(tm > 0)
    def _():
        bytes_wait(halo_out, ssem.at[HALO])

    for p in range(PARTS):
        bytes_wait(fetched.at[p, nc : nc + rows], ssem.at[TWIN + p])
        bytes_wait(fetched.at[p, 0 : nc - 2], ssem.at[FETCH + p])
    bytes_wait(sums_in.at[0 : nt - 1], ssem.at[SUMS])
    bytes_wait(peak_in.at[0 : nt - 1], ssem.at[PEAK])


def solution(mesh):
    nc, nt = mesh.shape["cells"], mesh.shape["tm"]

    def shards(urban, rural, urban_valid, rural_ids):
        hours, cells = urban.shape
        refs = rural_ids.shape[0]
        share = LAGS // nt
        groups, wide, slots, half = cells // GROUP, GROUP * refs, nc * CAP, nc // 2
        quads = groups // 4
        span, rows = hours // PARTS, cells // CAP
        vmem = pl.BlockSpec(memory_space=pltpu.VMEM)
        whole = pl.BlockSpec(memory_space=pl.ANY)
        return pl.pallas_call(
            functools.partial(kernel, nc, nt),
            out_shape=jax.ShapeDtypeStruct((share, refs, cells), F32),
            in_specs=[whole, whole, vmem, vmem],
            out_specs=vmem,
            scratch_shapes=[
                pltpu.VMEM((hours, cells), F32),
                pltpu.VMEM((hours, cells), F32),
                pltpu.VMEM((half, 2, cells), jnp.int32),
                pltpu.VMEM((half, 2, cells), jnp.int32),
                pltpu.VMEM((refs, cells), F32),
                pltpu.VMEM((nt, 8, cells), F32),
                pltpu.VMEM((hours // LAGS + 1, cells, LAGS), F32),
                pltpu.VMEM((cells, LAGS), BF16),
                pltpu.VMEM((cells, LAGS), BF16),
                pltpu.VMEM((PARTS, 2, half, CAP, span), BF16),
                pltpu.VMEM((2, half * CAP, cells), BF16),
                pltpu.VMEM((PARTS, nc + 2 * rows, CAP, span), BF16),
                pltpu.VMEM((cells * refs, slots + 2 * cells), BF16),
                pltpu.VMEM((cells, share, hours + LAGS), BF16),
                pltpu.VMEM((quads, 4, nt, wide, span + LAGS), BF16),
                pltpu.VMEM((groups, share, nt * wide), F32),
                pltpu.VMEM((quads, nt, 2, share, 2 * wide), F32),
                pltpu.VMEM((quads, nt, 2, share, 2 * wide), jnp.int16),
                pltpu.VMEM((nt, quads, 2, share, 2 * wide), jnp.int16),
                pltpu.VMEM((quads, 2, 1, 2 * wide), F32),
                pltpu.VMEM((nt, quads, 2, 1, 2 * wide), F32),
                pltpu.SemaphoreType.DMA((2,)),
                pltpu.SemaphoreType.DMA((KINDS,)),
                pltpu.SemaphoreType.DMA((KINDS,)),
            ],
            compiler_params=pltpu.CompilerParams(
                collective_id=0, has_side_effects=True, vmem_limit_bytes=52 * 1024 * 1024
            ),
        )(urban, rural, urban_valid.reshape(1, cells), rural_ids)

    in_specs = (P("tm", "cells"), P("tm", "cells"), P("cells"), P(None, "cells"))
    return jax.shard_map(
        shards, mesh=mesh, in_specs=in_specs, out_specs=P("tm", None, "cells"), check_vma=False
    )
```

```python
import functools

import jax
import jax.numpy as jnp
from jax import lax
from jax.experimental import pallas as pl
from jax.experimental.pallas import tpu as pltpu
from jax.sharding import PartitionSpec as P

LAGS = 128
EPSILON = 1e-05
CAP = 16
GROUP = 8
PARTS = 2
MESH = pl.DeviceIdType.MESH
F32 = jnp.float32
BF16 = jnp.bfloat16

REQ, STAT, HALO, SUMS, PEAK, TWIN, FETCH = 0, 1, 2, 3, 4, 5, 5 + PARTS
KINDS = 5 + 2 * PARTS
TOP = 32760.0


def iota(shape, axis):
    return lax.broadcasted_iota(jnp.int32, shape, axis)


def bytes_wait(ref, sem):
    pltpu.make_async_copy(ref, ref, sem).wait()


def kernel(
    nc, nt, urban_hbm, rural_hbm, valid_hbm, ids_hbm, out_ref,
    urban_ref, rural_ref, valid_ref, ids_ref, req_out, req_in, slot_rows, stats, ut, halo_out, halo_in,
    answer, choose, fetched, pick, toep, moved, part, kept, sums_out, sums_in, peak_out, peak_in, local_sem, ssem, rsem,
):
    hours, cells = urban_ref.shape
    refs = ids_ref.shape[0]
    share = LAGS // nt
    groups = cells // GROUP
    wide = GROUP * refs
    quads = groups // 4
    slots = nc * CAP
    half = nc // 2
    rows = cells // CAP
    span = hours // PARTS
    me = lax.axis_index("cells")
    tm = lax.axis_index("tm")
    side = me // half
    place = lax.rem(me, half)
    twin = (1 - side) * half + place

    def remote(kind, src, dst, **where):
        return pltpu.make_async_remote_copy(
            src_ref=src, dst_ref=dst, send_sem=ssem.at[kind], recv_sem=rsem.at[kind],
            device_id=where, device_id_type=MESH,
        )

    pairs = ((ids_hbm, ids_ref), (valid_hbm, valid_ref), (rural_hbm, rural_ref), (urban_hbm, urban_ref))
    copies = [pltpu.make_async_copy(src, dst, local_sem.at[i]) for i, (src, dst) in enumerate(pairs)]
    ids_in, valid_in, rural_in, urban_in = copies
    for copy in copies:
        copy.start()

    barrier = pltpu.get_barrier_semaphore()

    @pl.loop(1, nt)
    def _(d):
        pl.semaphore_signal(barrier, inc=1, device_id={"tm": lax.rem(tm + d, nt)}, device_id_type=MESH)

    pl.semaphore_signal(barrier, inc=1, device_id={"cells": twin}, device_id_type=MESH)

    @pl.loop(1, half)
    def _(d):
        peer = side * half + lax.rem(place + d, half)
        pl.semaphore_signal(barrier, inc=1, device_id={"cells": peer}, device_id_type=MESH)

    ids_in.wait()
    ids = ids_ref[...]
    owner = (ids >> 7).astype(F32)
    local = (ids & 127).astype(F32)
    upper = jnp.where(owner >= half, 1.0, 0.0)
    away = jnp.where(upper == side.astype(F32), 0.0, 1.0)
    home = (owner - half * upper) * 2.0 + away
    home_i = iota((nc, cells), 0).astype(F32)
    belongs = [jnp.where(home[k : k + 1] == home_i, 1.0, 0.0) for k in range(refs)]
    earlier = iota((cells, 2 * cells), 0) < iota((cells, 2 * cells), 1)
    counts = jnp.dot(
        jnp.concatenate(belongs, axis=0).astype(BF16), jnp.where(earlier, 1.0, 0.0).astype(BF16),
        preferred_element_type=F32,
    )
    before = jnp.zeros((nc, cells), F32)
    rank_i = iota((cells, cells), 0).astype(F32)
    asks = jnp.zeros((nc, cells), F32)
    for k in range(refs):
        count = counts[k * nc : (k + 1) * nc]
        rank = jnp.sum(belongs[k] * (count[:, 0:cells] + before), axis=0, keepdims=True)
        before += count[:, cells : 2 * cells]
        wish = jnp.where(rank == rank_i, local[k : k + 1], 0.0).astype(BF16)
        asks += lax.dot_general(
            belongs[k].astype(BF16), wish, (((1,), (1,)), ((), ())), preferred_element_type=F32
        )
        slot = home[k : k + 1] * CAP + rank
        slot = jnp.where(owner[k : k + 1] == me.astype(F32), slots + local[k : k + 1], slot)
        slot = jnp.where(owner[k : k + 1] == twin.astype(F32), slots + cells + local[k : k + 1], slot)
        slot_rows[k : k + 1] = slot
    asks = asks.astype(jnp.int32)
    for q in range(half):
        req_out[q] = asks[2 * q : 2 * q + 2]

    valid_in.wait()
    valid = valid_ref[...].astype(F32)
    hour = (tm * hours + iota((hours, cells), 0)).astype(F32)
    mask = (hour < valid).astype(F32)
    mine = stats.at[tm]
    rural_in.wait()
    rural = rural_ref[...]
    mine[2:3] = jnp.sum(rural, axis=0, keepdims=True)
    mine[3:4] = jnp.sum(rural * rural, axis=0, keepdims=True)
    urban_in.wait()
    urban = urban_ref[...]
    mine[0:1] = jnp.sum(urban * mask, axis=0, keepdims=True)
    mine[1:2] = jnp.sum(urban * urban * mask, axis=0, keepdims=True)
    mine[4:8] = jnp.zeros((4, cells), F32)

    pl.semaphore_wait(barrier, half - 1 + 1 + nt - 1)

    @pl.loop(1, nt)
    def _(d):
        remote(STAT, stats.at[tm], stats.at[tm], tm=lax.rem(tm + d, nt)).start()


    @pl.loop(1, half)
    def _(d):
        other = lax.rem(place + d, half)
        remote(REQ, req_out.at[other], req_in.at[place], cells=side * half + other).start()

    req_in[place] = jnp.zeros((2, cells), jnp.int32)

    lane = iota((GROUP, cells), 1)
    row = iota((GROUP, cells), 0)
    lane_w = iota((wide, cells), 1)

    @pl.loop(0, groups, unroll=4)
    def _(g):
        one = lane == GROUP * g + row
        table = slot_rows[...]
        each = [jnp.where(one, table[k : k + 1], 0.0) for k in range(refs)]
        slot = jnp.sum(jnp.concatenate(each, axis=0), axis=1, keepdims=True).astype(jnp.int32)
        begin = pl.multiple_of(g * wide, wide)
        for j in range(slots // cells + 2):
            hit = slot == lane_w + j * cells
            pick[pl.ds(begin, wide), j * cells : (j + 1) * cells] = jnp.where(hit, 1.0, 0.0).astype(BF16)

    for p in range(PARTS):
        fetched[p, pl.ds(2 * place, 2)] = jnp.zeros((2, CAP, span), BF16)

    bytes_wait(stats.at[0 : nt - 1], rsem.at[STAT])
    total = stats[0]
    for i in range(1, nt):
        total += stats[i]

    def finish(series, first, second, n, keep):
        average = first / n
        spread = second / n - average * average
        return (series - average) * lax.rsqrt(spread + EPSILON) * keep

    def settle(p):
        rural_z = finish(rural_ref[p * span : (p + 1) * span], total[2:3], total[3:4], F32(hours * nt), F32(1.0))
        turned = jnp.transpose(rural_z).astype(BF16)
        fetched[p, nc : nc + rows] = turned.reshape(rows, CAP, span)
        remote(
            TWIN + p, fetched.at[p, nc : nc + rows], fetched.at[p, nc + rows : nc + 2 * rows], cells=twin
        ).start()
    settle(0)

    bytes_wait(req_in.at[0 : half - 1], rsem.at[REQ])
    batch = min(8, half)
    chunks = half // batch
    lane_c = iota((CAP, cells), 1)
    row_c = iota((CAP, cells), 0)
    here = lane_c == row_c
    height = batch * CAP
    lane_h = iota((height, cells), 1)

    def respond(rel, p, q):
        block = fetched[p, nc + rel * rows : nc + (rel + 1) * rows].reshape(cells, span)
        begin = pl.multiple_of(q * height, height)
        chosen = jnp.dot(choose[rel, pl.ds(begin, height), :], block, preferred_element_type=F32)
        answer[p, rel, pl.ds(q * batch, batch)] = chosen.astype(BF16).reshape(batch, CAP, span)

        @pl.loop(0, batch)
        def _(s):
            other = q * batch + s

            @pl.when(other != place)
            def _():
                remote(
                    FETCH + p, answer.at[p, rel, other], fetched.at[p, 2 * place + rel], cells=side * half + other
                ).start()

    def respond_all(rel, p):
        @pl.loop(0, chunks)
        def _(step):
            respond(rel, p, lax.rem(place // batch + step, chunks))

    def prepare(rel, q):
        begin = pl.multiple_of(q * height, height)
        columns = []
        for s in range(batch):
            asked = req_in[q * batch + s][rel : rel + 1].astype(F32)
            columns.append(jnp.sum(jnp.where(here, asked, 0.0), axis=1, keepdims=True))
        column = jnp.concatenate(columns, axis=0).astype(jnp.int32)
        choose[rel, pl.ds(begin, height), :] = jnp.where(column == lane_h, 1.0, 0.0).astype(BF16)

    @pl.loop(0, chunks)
    def _(step):
        q = lax.rem(place // batch + step, chunks)
        prepare(0, q)
        respond(0, 0, q)

    for p in range(1, PARTS):
        settle(p)
    @pl.loop(0, chunks)
    def _(q):
        prepare(1, q)

    urban_z = finish(urban_ref[...], total[0:1], total[1:2], valid, mask)
    for j in range(hours // LAGS):
        ut[j] = jnp.transpose(urban_z[j * LAGS : (j + 1) * LAGS])
    halo_out[...] = ut[0].astype(BF16)

    @pl.when(tm > 0)
    def _():
        remote(HALO, halo_out, halo_in, tm=tm - 1).start()

    tiles = hours // LAGS
    lane8 = iota((8, LAGS), 1)
    row8 = iota((8, LAGS), 0)

    def build(first, last):
        @pl.loop(first, last, unroll=8)
        def _(c):
            wave = [jnp.broadcast_to(ut[j, pl.ds(c, 1), :], (8, LAGS)) for j in range(tiles + 1)]
            for pair in range(share // 16):
                halves = []
                for a in (2 * pair, 2 * pair + 1):
                    shift = LAGS - share + 1 + 8 * a
                    turned = [pltpu.roll(x, shift, 1, stride=1, stride_axis=0) for x in wave]
                    turned.append(jnp.zeros((8, LAGS), F32))
                    upper = lane8 >= row8 + shift
                    halves.append([jnp.where(upper, turned[j + 1], turned[j]) for j in range(tiles + 1)])
                for j in range(tiles + 1):
                    both = jnp.concatenate([halves[0][j], halves[1][j]], axis=0).astype(BF16)
                    toep[c, 16 * pair : 16 * pair + 16, j * LAGS : (j + 1) * LAGS] = both

    bytes_wait(fetched.at[0, nc + rows : nc + 2 * rows], rsem.at[TWIN + 0])
    respond_all(1, 0)
    respond_all(0, 1)
    bytes_wait(fetched.at[1, nc + rows : nc + 2 * rows], rsem.at[TWIN + 1])
    respond_all(1, 1)
    @pl.when(tm < nt - 1)
    def _():
        bytes_wait(halo_in, rsem.at[HALO])
        ut[hours // LAGS] = halo_in[...].astype(F32)

    @pl.when(tm == nt - 1)
    def _():
        ut[hours // LAGS] = jnp.zeros((cells, LAGS), F32)

    build(0, cells)
    column_of = lax.rem(iota((share, nt * wide), 1), GROUP)
    lane_t = iota((4 * wide, LAGS), 1)
    lane_s = iota((share, 2 * wide), 1)
    reach = span + LAGS
    for p in range(PARTS):
        bytes_wait(fetched.at[p, 0 : nc - 2], rsem.at[FETCH + p])

        for lot in ([range(quads)] if p < PARTS - 1 else [range(0, 2), range(2, quads)]):
            for quad in lot:
                begin = quad * 4 * wide
                chosen = jnp.dot(
                    pick[begin : begin + 4 * wide, :],
                    fetched[p].reshape(slots + 2 * cells, span),
                    preferred_element_type=F32,
                )
                pieces = [chosen[:, j * LAGS : (j + 1) * LAGS] for j in range(span // LAGS)]
                none = jnp.zeros((4 * wide, LAGS), F32)
                for a in range(nt):
                    shift = share * a
                    turned = [none] + [pltpu.roll(x, shift, 1) if a else x for x in pieces] + [none]
                    for j in range(span // LAGS + 1):
                        piece = jnp.where(lane_t >= shift, turned[j + 1], turned[j]) if a else turned[j + 1]
                        piece = piece.astype(BF16)
                        for i in range(4):
                            moved[quad, i, a, :, j * LAGS : (j + 1) * LAGS] = piece[i * wide : (i + 1) * wide]
            for quad in lot:
                totals = []
                for i in range(4):
                    g = 4 * quad + i
                    left = toep[GROUP * g : GROUP * (g + 1), :, p * span : p * span + reach].reshape(GROUP * share, reach)
                    sums = lax.dot_general(
                        left, moved[quad, i].reshape(nt * wide, reach), (((1,), (1,)), ((), ())), preferred_element_type=F32
                    )
                    total = sums[0:share]
                    for c in range(1, GROUP):
                        total = jnp.where(column_of == c, sums[c * share : (c + 1) * share], total)
                    if p:
                        total += part[g]
                    if p < PARTS - 1:
                        part[g] = total
                    totals.append(total)
                if p == PARTS - 1:
                    for h in range(2):
                        even, odd = totals[2 * h], totals[2 * h + 1]
                        blocks = []
                        for a in range(nt):
                            at = (a // 2) * 2 * wide
                            x, y = even[:, at : at + 2 * wide], odd[:, at : at + 2 * wide]
                            if a % 2:
                                x = pltpu.roll(x, wide, 1)
                            else:
                                y = pltpu.roll(y, wide, 1)
                            blocks.append(jnp.where(lane_s < wide, x, y))
                        peak = jnp.full((1, 2 * wide), 1e-30, F32)
                        for block in blocks:
                            peak = jnp.maximum(peak, jnp.max(jnp.abs(block), axis=0, keepdims=True))
                        peak_out[quad, h] = peak
                        scale = TOP / peak
                        for a in range(nt):
                            kept[quad, a, h] = blocks[a]
                            sums_out[quad, a, h] = (
                                jnp.floor(blocks[a] * scale + 0.5).astype(jnp.int32).astype(jnp.int16)
                            )

                    for d in list(range(nt // 2, nt)) + list(range(1, nt // 2)):
                        peer = tm ^ d
                        remote(SUMS, sums_out.at[quad, peer], sums_in.at[tm, quad], tm=peer).start()
                        remote(PEAK, peak_out.at[quad], peak_in.at[tm, quad], tm=peer).start()

    sums_in[tm] = jnp.zeros((quads, 2, share, 2 * wide), jnp.int16)
    peak_in[tm] = jnp.zeros((quads, 2, 1, 2 * wide), F32)
    bytes_wait(sums_in.at[0 : nt - 1], rsem.at[SUMS])
    bytes_wait(peak_in.at[0 : nt - 1], rsem.at[PEAK])

    whole = []
    for quad in range(quads):
        for h in range(2):
            total = kept[quad, tm, h]
            for i in range(nt):
                total += sums_in[i, quad, h].astype(jnp.int32).astype(F32) * (peak_in[i, quad, h] * (1.0 / TOP))
            whole.append(total)
    lag = tm * share + (share - 1) - iota((share, cells), 0)
    overlap = (valid_ref[...] - lag).astype(F32)
    place_o = iota((share, cells), 1) // GROUP
    for k in range(refs):
        result = jnp.zeros((share, cells), F32)
        for g in range(groups):
            shift = (GROUP * g - wide * (g % 2) - GROUP * k) % cells
            piece = whole[g // 2]
            if shift:
                piece = pltpu.roll(piece, shift, 1)
            result = jnp.where(place_o == g, piece, result)
        result = result / overlap
        for i in range(share):
            out_ref[share - 1 - i, k : k + 1, :] = result[i : i + 1]

    bytes_wait(req_in.at[0 : half - 1], ssem.at[REQ])
    bytes_wait(stats.at[0 : nt - 1], ssem.at[STAT])

    @pl.when(tm > 0)
    def _():
        bytes_wait(halo_out, ssem.at[HALO])

    for p in range(PARTS):
        bytes_wait(fetched.at[p, nc : nc + rows], ssem.at[TWIN + p])
        bytes_wait(fetched.at[p, 0 : nc - 2], ssem.at[FETCH + p])
    bytes_wait(sums_in.at[0 : nt - 1], ssem.at[SUMS])
    bytes_wait(peak_in.at[0 : nt - 1], ssem.at[PEAK])


def solution(mesh):
    nc, nt = mesh.shape["cells"], mesh.shape["tm"]

    def shards(urban, rural, urban_valid, rural_ids):
        hours, cells = urban.shape
        refs = rural_ids.shape[0]
        share = LAGS // nt
        groups, wide, slots, half = cells // GROUP, GROUP * refs, nc * CAP, nc // 2
        quads = groups // 4
        span, rows = hours // PARTS, cells // CAP
        return pl.pallas_call(
            functools.partial(kernel, nc, nt),
            out_shape=jax.ShapeDtypeStruct((share, refs, cells), F32),
            in_specs=[pl.BlockSpec(memory_space=pltpu.HBM)] * 4,
            out_specs=pl.BlockSpec(memory_space=pltpu.VMEM),
            scratch_shapes=[
                pltpu.VMEM((hours, cells), F32),
                pltpu.VMEM((hours, cells), F32),
                pltpu.VMEM((1, cells), jnp.int32),
                pltpu.VMEM((refs, cells), jnp.int32),
                pltpu.VMEM((half, 2, cells), jnp.int32),
                pltpu.VMEM((half, 2, cells), jnp.int32),
                pltpu.VMEM((refs, cells), F32),
                pltpu.VMEM((nt, 8, cells), F32),
                pltpu.VMEM((hours // LAGS + 1, cells, LAGS), F32),
                pltpu.VMEM((cells, LAGS), BF16),
                pltpu.VMEM((cells, LAGS), BF16),
                pltpu.VMEM((PARTS, 2, half, CAP, span), BF16),
                pltpu.VMEM((2, half * CAP, cells), BF16),
                pltpu.VMEM((PARTS, nc + 2 * rows, CAP, span), BF16),
                pltpu.VMEM((cells * refs, slots + 2 * cells), BF16),
                pltpu.VMEM((cells, share, hours + LAGS), BF16),
                pltpu.VMEM((quads, 4, nt, wide, span + LAGS), BF16),
                pltpu.VMEM((groups, share, nt * wide), F32),
                pltpu.VMEM((quads, nt, 2, share, 2 * wide), F32),
                pltpu.VMEM((quads, nt, 2, share, 2 * wide), jnp.int16),
                pltpu.VMEM((nt, quads, 2, share, 2 * wide), jnp.int16),
                pltpu.VMEM((quads, 2, 1, 2 * wide), F32),
                pltpu.VMEM((nt, quads, 2, 1, 2 * wide), F32),
                pltpu.SemaphoreType.DMA((4,)),
                pltpu.SemaphoreType.DMA((KINDS,)),
                pltpu.SemaphoreType.DMA((KINDS,)),
            ],
            compiler_params=pltpu.CompilerParams(
                collective_id=0, has_side_effects=True, vmem_limit_bytes=62 * 1024 * 1024
            ),
        )(urban, rural, urban_valid.reshape(1, cells), rural_ids)

    in_specs = (P("tm", "cells"), P("tm", "cells"), P("cells"), P(None, "cells"))
    return jax.shard_map(
        shards, mesh=mesh, in_specs=in_specs, out_specs=P("tm", None, "cells"), check_vma=False
    )
```

```python
import functools

import jax
import jax.numpy as jnp
from jax import lax
from jax.experimental import pallas as pl
from jax.experimental.pallas import tpu as pltpu
from jax.sharding import PartitionSpec as P

LAGS = 128
EPSILON = 1e-05
CAP = 16
GROUP = 8
PARTS = 2
MESH = pl.DeviceIdType.MESH
F32 = jnp.float32
BF16 = jnp.bfloat16

REQ, STAT, HALO, SUMS, PEAK, TWIN, FETCH = 0, 1, 2, 3, 4, 5, 5 + PARTS
KINDS = 5 + 2 * PARTS
TOP = 32760.0


def iota(shape, axis):
    return lax.broadcasted_iota(jnp.int32, shape, axis)


def bytes_wait(ref, sem):
    pltpu.make_async_copy(ref, ref, sem).wait()


def kernel(
    nc, nt, urban_hbm, rural_hbm, valid_hbm, ids_hbm, out_ref,
    urban_ref, rural_ref, valid_ref, ids_ref, req_out, req_in, slot_rows, stats, ut, halo_out, halo_in,
    answer, choose, fetched, pick, toep, moved, part, kept, sums_out, sums_in, peak_out, peak_in, local_sem, ssem, rsem,
):
    hours, cells = urban_ref.shape
    refs = ids_ref.shape[0]
    share = LAGS // nt
    groups = cells // GROUP
    wide = GROUP * refs
    quads = groups // 4
    slots = nc * CAP
    half = nc // 2
    rows = cells // CAP
    span = hours // PARTS
    me = lax.axis_index("cells")
    tm = lax.axis_index("tm")
    side = me // half
    place = lax.rem(me, half)
    twin = (1 - side) * half + place

    def remote(kind, src, dst, **where):
        return pltpu.make_async_remote_copy(
            src_ref=src, dst_ref=dst, send_sem=ssem.at[kind], recv_sem=rsem.at[kind],
            device_id=where, device_id_type=MESH,
        )

    pairs = ((ids_hbm, ids_ref), (valid_hbm, valid_ref), (rural_hbm, rural_ref), (urban_hbm, urban_ref))
    copies = [pltpu.make_async_copy(src, dst, local_sem.at[i]) for i, (src, dst) in enumerate(pairs)]
    ids_in, valid_in, rural_in, urban_in = copies
    for copy in copies:
        copy.start()

    barrier = pltpu.get_barrier_semaphore()

    @pl.loop(1, nt)
    def _(d):
        pl.semaphore_signal(barrier, inc=1, device_id={"tm": lax.rem(tm + d, nt)}, device_id_type=MESH)

    pl.semaphore_signal(barrier, inc=1, device_id={"cells": twin}, device_id_type=MESH)

    @pl.loop(1, half)
    def _(d):
        peer = side * half + lax.rem(place + d, half)
        pl.semaphore_signal(barrier, inc=1, device_id={"cells": peer}, device_id_type=MESH)

    ids_in.wait()
    ids = ids_ref[...]
    owner = (ids >> 7).astype(F32)
    local = (ids & 127).astype(F32)
    upper = jnp.where(owner >= half, 1.0, 0.0)
    away = jnp.where(upper == side.astype(F32), 0.0, 1.0)
    home = (owner - half * upper) * 2.0 + away
    home_i = iota((nc, cells), 0).astype(F32)
    belongs = [jnp.where(home[k : k + 1] == home_i, 1.0, 0.0) for k in range(refs)]
    earlier = iota((cells, 2 * cells), 0) < iota((cells, 2 * cells), 1)
    counts = jnp.dot(
        jnp.concatenate(belongs, axis=0).astype(BF16), jnp.where(earlier, 1.0, 0.0).astype(BF16),
        preferred_element_type=F32,
    )
    before = jnp.zeros((nc, cells), F32)
    rank_i = iota((cells, cells), 0).astype(F32)
    asks = jnp.zeros((nc, cells), F32)
    for k in range(refs):
        count = counts[k * nc : (k + 1) * nc]
        rank = jnp.sum(belongs[k] * (count[:, 0:cells] + before), axis=0, keepdims=True)
        before += count[:, cells : 2 * cells]
        wish = jnp.where(rank == rank_i, local[k : k + 1], 0.0).astype(BF16)
        asks += lax.dot_general(
            belongs[k].astype(BF16), wish, (((1,), (1,)), ((), ())), preferred_element_type=F32
        )
        slot = home[k : k + 1] * CAP + rank
        slot = jnp.where(owner[k : k + 1] == me.astype(F32), slots + local[k : k + 1], slot)
        slot = jnp.where(owner[k : k + 1] == twin.astype(F32), slots + cells + local[k : k + 1], slot)
        slot_rows[k : k + 1] = slot
    asks = asks.astype(jnp.int32)
    for q in range(half):
        req_out[q] = asks[2 * q : 2 * q + 2]

    valid_in.wait()
    valid = valid_ref[...].astype(F32)
    hour = (tm * hours + iota((hours, cells), 0)).astype(F32)
    mask = (hour < valid).astype(F32)
    mine = stats.at[tm]
    rural_in.wait()
    rural = rural_ref[...]
    mine[2:3] = jnp.sum(rural, axis=0, keepdims=True)
    mine[3:4] = jnp.sum(rural * rural, axis=0, keepdims=True)
    urban_in.wait()
    urban = urban_ref[...]
    mine[0:1] = jnp.sum(urban * mask, axis=0, keepdims=True)
    mine[1:2] = jnp.sum(urban * urban * mask, axis=0, keepdims=True)
    mine[4:8] = jnp.zeros((4, cells), F32)

    pl.semaphore_wait(barrier, half - 1 + 1 + nt - 1)

    @pl.loop(1, nt)
    def _(d):
        remote(STAT, stats.at[tm], stats.at[tm], tm=lax.rem(tm + d, nt)).start()


    @pl.loop(1, half)
    def _(d):
        other = lax.rem(place + d, half)
        remote(REQ, req_out.at[other], req_in.at[place], cells=side * half + other).start()

    req_in[place] = jnp.zeros((2, cells), jnp.int32)

    lane = iota((GROUP, cells), 1)
    row = iota((GROUP, cells), 0)
    lane_w = iota((wide, cells), 1)

    @pl.loop(0, groups, unroll=4)
    def _(g):
        one = lane == GROUP * g + row
        table = slot_rows[...]
        each = [jnp.where(one, table[k : k + 1], 0.0) for k in range(refs)]
        slot = jnp.sum(jnp.concatenate(each, axis=0), axis=1, keepdims=True).astype(jnp.int32)
        begin = pl.multiple_of(g * wide, wide)
        for j in range(slots // cells + 2):
            hit = slot == lane_w + j * cells
            pick[pl.ds(begin, wide), j * cells : (j + 1) * cells] = jnp.where(hit, 1.0, 0.0).astype(BF16)

    for p in range(PARTS):
        fetched[p, pl.ds(2 * place, 2)] = jnp.zeros((2, CAP, span), BF16)

    bytes_wait(stats.at[0 : nt - 1], rsem.at[STAT])
    total = stats[0]
    for i in range(1, nt):
        total += stats[i]

    def finish(series, first, second, n, keep):
        average = first / n
        spread = second / n - average * average
        return (series - average) * lax.rsqrt(spread + EPSILON) * keep

    def settle(p):
        rural_z = finish(rural_ref[p * span : (p + 1) * span], total[2:3], total[3:4], F32(hours * nt), F32(1.0))
        turned = jnp.transpose(rural_z).astype(BF16)
        fetched[p, nc : nc + rows] = turned.reshape(rows, CAP, span)
        remote(
            TWIN + p, fetched.at[p, nc : nc + rows], fetched.at[p, nc + rows : nc + 2 * rows], cells=twin
        ).start()
    settle(0)

    bytes_wait(req_in.at[0 : half - 1], rsem.at[REQ])
    batch = min(8, half)
    chunks = half // batch
    lane_c = iota((CAP, cells), 1)
    row_c = iota((CAP, cells), 0)
    here = lane_c == row_c
    height = batch * CAP
    lane_h = iota((height, cells), 1)

    def respond(rel, p, q):
        block = fetched[p, nc + rel * rows : nc + (rel + 1) * rows].reshape(cells, span)
        begin = pl.multiple_of(q * height, height)
        chosen = jnp.dot(choose[rel, pl.ds(begin, height), :], block, preferred_element_type=F32)
        answer[p, rel, pl.ds(q * batch, batch)] = chosen.astype(BF16).reshape(batch, CAP, span)

        @pl.loop(0, batch)
        def _(s):
            other = q * batch + s

            @pl.when(other != place)
            def _():
                remote(
                    FETCH + p, answer.at[p, rel, other], fetched.at[p, 2 * place + rel], cells=side * half + other
                ).start()

    def respond_all(rel, p):
        @pl.loop(0, chunks)
        def _(step):
            respond(rel, p, lax.rem(place // batch + step, chunks))

    def prepare(rel, q):
        begin = pl.multiple_of(q * height, height)
        columns = []
        for s in range(batch):
            asked = req_in[q * batch + s][rel : rel + 1].astype(F32)
            columns.append(jnp.sum(jnp.where(here, asked, 0.0), axis=1, keepdims=True))
        column = jnp.concatenate(columns, axis=0).astype(jnp.int32)
        choose[rel, pl.ds(begin, height), :] = jnp.where(column == lane_h, 1.0, 0.0).astype(BF16)

    @pl.loop(0, chunks)
    def _(step):
        q = lax.rem(place // batch + step, chunks)
        prepare(0, q)
        respond(0, 0, q)

    for p in range(1, PARTS):
        settle(p)
    @pl.loop(0, chunks)
    def _(q):
        prepare(1, q)

    urban_z = finish(urban_ref[...], total[0:1], total[1:2], valid, mask)
    for j in range(hours // LAGS):
        ut[j] = jnp.transpose(urban_z[j * LAGS : (j + 1) * LAGS])
    halo_out[...] = ut[0].astype(BF16)

    @pl.when(tm > 0)
    def _():
        remote(HALO, halo_out, halo_in, tm=tm - 1).start()

    tiles = hours // LAGS
    lane8 = iota((8, LAGS), 1)
    row8 = iota((8, LAGS), 0)

    def build(first, last):
        @pl.loop(first, last, unroll=8)
        def _(c):
            wave = [jnp.broadcast_to(ut[j, pl.ds(c, 1), :], (8, LAGS)) for j in range(tiles + 1)]
            for pair in range(share // 16):
                halves = []
                for a in (2 * pair, 2 * pair + 1):
                    shift = LAGS - share + 1 + 8 * a
                    turned = [pltpu.roll(x, shift, 1, stride=1, stride_axis=0) for x in wave]
                    turned.append(jnp.zeros((8, LAGS), F32))
                    upper = lane8 >= row8 + shift
                    halves.append([jnp.where(upper, turned[j + 1], turned[j]) for j in range(tiles + 1)])
                for j in range(tiles + 1):
                    both = jnp.concatenate([halves[0][j], halves[1][j]], axis=0).astype(BF16)
                    toep[c, 16 * pair : 16 * pair + 16, j * LAGS : (j + 1) * LAGS] = both

    bytes_wait(fetched.at[0, nc + rows : nc + 2 * rows], rsem.at[TWIN + 0])
    respond_all(1, 0)
    respond_all(0, 1)
    bytes_wait(fetched.at[1, nc + rows : nc + 2 * rows], rsem.at[TWIN + 1])
    respond_all(1, 1)
    @pl.when(tm < nt - 1)
    def _():
        bytes_wait(halo_in, rsem.at[HALO])
        ut[hours // LAGS] = halo_in[...].astype(F32)

    @pl.when(tm == nt - 1)
    def _():
        ut[hours // LAGS] = jnp.zeros((cells, LAGS), F32)

    build(0, cells)
    column_of = lax.rem(iota((share, nt * wide), 1), GROUP)
    lane_t = iota((4 * wide, LAGS), 1)
    lane_s = iota((share, 2 * wide), 1)
    reach = span + LAGS
    for p in range(PARTS):
        bytes_wait(fetched.at[p, 0 : nc - 2], rsem.at[FETCH + p])

        for lot in ([range(quads)] if p < PARTS - 1 else [[q] for q in range(quads)]):
            for quad in lot:
                begin = quad * 4 * wide
                chosen = jnp.dot(
                    pick[begin : begin + 4 * wide, :],
                    fetched[p].reshape(slots + 2 * cells, span),
                    preferred_element_type=F32,
                )
                pieces = [chosen[:, j * LAGS : (j + 1) * LAGS] for j in range(span // LAGS)]
                none = jnp.zeros((4 * wide, LAGS), F32)
                for a in range(nt):
                    shift = share * a
                    turned = [none] + [pltpu.roll(x, shift, 1) if a else x for x in pieces] + [none]
                    for j in range(span // LAGS + 1):
                        piece = jnp.where(lane_t >= shift, turned[j + 1], turned[j]) if a else turned[j + 1]
                        piece = piece.astype(BF16)
                        for i in range(4):
                            moved[quad, i, a, :, j * LAGS : (j + 1) * LAGS] = piece[i * wide : (i + 1) * wide]
            for quad in lot:
                totals = []
                for i in range(4):
                    g = 4 * quad + i
                    left = toep[GROUP * g : GROUP * (g + 1), :, p * span : p * span + reach].reshape(GROUP * share, reach)
                    sums = lax.dot_general(
                        left, moved[quad, i].reshape(nt * wide, reach), (((1,), (1,)), ((), ())), preferred_element_type=F32
                    )
                    total = sums[0:share]
                    for c in range(1, GROUP):
                        total = jnp.where(column_of == c, sums[c * share : (c + 1) * share], total)
                    if p:
                        total += part[g]
                    if p < PARTS - 1:
                        part[g] = total
                    totals.append(total)
                if p == PARTS - 1:
                    for h in range(2):
                        even, odd = totals[2 * h], totals[2 * h + 1]
                        blocks = []
                        for a in range(nt):
                            at = (a // 2) * 2 * wide
                            x, y = even[:, at : at + 2 * wide], odd[:, at : at + 2 * wide]
                            if a % 2:
                                x = pltpu.roll(x, wide, 1)
                            else:
                                y = pltpu.roll(y, wide, 1)
                            blocks.append(jnp.where(lane_s < wide, x, y))
                        peak = jnp.full((1, 2 * wide), 1e-30, F32)
                        for block in blocks:
                            peak = jnp.maximum(peak, jnp.max(jnp.abs(block), axis=0, keepdims=True))
                        peak_out[quad, h] = peak
                        scale = TOP / peak
                        for a in range(nt):
                            kept[quad, a, h] = blocks[a]
                            sums_out[quad, a, h] = (
                                jnp.floor(blocks[a] * scale + 0.5).astype(jnp.int32).astype(jnp.int16)
                            )

                    for d in list(range(nt // 2, nt)) + list(range(1, nt // 2)):
                        peer = tm ^ d
                        remote(SUMS, sums_out.at[quad, peer], sums_in.at[tm, quad], tm=peer).start()
                        remote(PEAK, peak_out.at[quad], peak_in.at[tm, quad], tm=peer).start()

    sums_in[tm] = jnp.zeros((quads, 2, share, 2 * wide), jnp.int16)
    peak_in[tm] = jnp.zeros((quads, 2, 1, 2 * wide), F32)
    bytes_wait(sums_in.at[0 : nt - 1], rsem.at[SUMS])
    bytes_wait(peak_in.at[0 : nt - 1], rsem.at[PEAK])

    whole = []
    for quad in range(quads):
        for h in range(2):
            total = kept[quad, tm, h]
            for i in range(nt):
                total += sums_in[i, quad, h].astype(jnp.int32).astype(F32) * (peak_in[i, quad, h] * (1.0 / TOP))
            whole.append(total)
    lag = tm * share + (share - 1) - iota((share, cells), 0)
    overlap = (valid_ref[...] - lag).astype(F32)
    place_o = iota((share, cells), 1) // GROUP
    for k in range(refs):
        result = jnp.zeros((share, cells), F32)
        for g in range(groups):
            shift = (GROUP * g - wide * (g % 2) - GROUP * k) % cells
            piece = whole[g // 2]
            if shift:
                piece = pltpu.roll(piece, shift, 1)
            result = jnp.where(place_o == g, piece, result)
        result = result / overlap
        for i in range(share):
            out_ref[share - 1 - i, k : k + 1, :] = result[i : i + 1]

    bytes_wait(req_in.at[0 : half - 1], ssem.at[REQ])
    bytes_wait(stats.at[0 : nt - 1], ssem.at[STAT])

    @pl.when(tm > 0)
    def _():
        bytes_wait(halo_out, ssem.at[HALO])

    for p in range(PARTS):
        bytes_wait(fetched.at[p, nc : nc + rows], ssem.at[TWIN + p])
        bytes_wait(fetched.at[p, 0 : nc - 2], ssem.at[FETCH + p])
    bytes_wait(sums_in.at[0 : nt - 1], ssem.at[SUMS])
    bytes_wait(peak_in.at[0 : nt - 1], ssem.at[PEAK])


def solution(mesh):
    nc, nt = mesh.shape["cells"], mesh.shape["tm"]

    def shards(urban, rural, urban_valid, rural_ids):
        hours, cells = urban.shape
        refs = rural_ids.shape[0]
        share = LAGS // nt
        groups, wide, slots, half = cells // GROUP, GROUP * refs, nc * CAP, nc // 2
        quads = groups // 4
        span, rows = hours // PARTS, cells // CAP
        return pl.pallas_call(
            functools.partial(kernel, nc, nt),
            out_shape=jax.ShapeDtypeStruct((share, refs, cells), F32),
            in_specs=[pl.BlockSpec(memory_space=pltpu.HBM)] * 4,
            out_specs=pl.BlockSpec(memory_space=pltpu.VMEM),
            scratch_shapes=[
                pltpu.VMEM((hours, cells), F32),
                pltpu.VMEM((hours, cells), F32),
                pltpu.VMEM((1, cells), jnp.int32),
                pltpu.VMEM((refs, cells), jnp.int32),
                pltpu.VMEM((half, 2, cells), jnp.int32),
                pltpu.VMEM((half, 2, cells), jnp.int32),
                pltpu.VMEM((refs, cells), F32),
                pltpu.VMEM((nt, 8, cells), F32),
                pltpu.VMEM((hours // LAGS + 1, cells, LAGS), F32),
                pltpu.VMEM((cells, LAGS), BF16),
                pltpu.VMEM((cells, LAGS), BF16),
                pltpu.VMEM((PARTS, 2, half, CAP, span), BF16),
                pltpu.VMEM((2, half * CAP, cells), BF16),
                pltpu.VMEM((PARTS, nc + 2 * rows, CAP, span), BF16),
                pltpu.VMEM((cells * refs, slots + 2 * cells), BF16),
                pltpu.VMEM((cells, share, hours + LAGS), BF16),
                pltpu.VMEM((quads, 4, nt, wide, span + LAGS), BF16),
                pltpu.VMEM((groups, share, nt * wide), F32),
                pltpu.VMEM((quads, nt, 2, share, 2 * wide), F32),
                pltpu.VMEM((quads, nt, 2, share, 2 * wide), jnp.int16),
                pltpu.VMEM((nt, quads, 2, share, 2 * wide), jnp.int16),
                pltpu.VMEM((quads, 2, 1, 2 * wide), F32),
                pltpu.VMEM((nt, quads, 2, 1, 2 * wide), F32),
                pltpu.SemaphoreType.DMA((4,)),
                pltpu.SemaphoreType.DMA((KINDS,)),
                pltpu.SemaphoreType.DMA((KINDS,)),
            ],
            compiler_params=pltpu.CompilerParams(
                collective_id=0, has_side_effects=True, vmem_limit_bytes=62 * 1024 * 1024
            ),
        )(urban, rural, urban_valid.reshape(1, cells), rural_ids)

    in_specs = (P("tm", "cells"), P("tm", "cells"), P("cells"), P(None, "cells"))
    return jax.shard_map(
        shards, mesh=mesh, in_specs=in_specs, out_specs=P("tm", None, "cells"), check_vma=False
    )
```
